32 devices in a mesh: fsdp: 8 (over y, x, core), dp: 4 (over z).
Axes of the slice: x: 2, y: 2, z: 4, core: 2. Of those that a mesh axis runs over, the one named last changes fastest.
Arguments:
- inputs: bfloat16 [8192, 1536], P(('fsdp', 'dp')), may hold values from -6 to 6
- cotangent: bfloat16 [8192, 1536], P(('fsdp', 'dp')), may hold values from -6 to 6
- needle: int32 [8192], P(('fsdp', 'dp')), may hold values from 0 to 1
- qkv_weight: float32 [1536, 4608], P(('fsdp', 'dp')), may hold values from -0.15625 to 0.15625
- qkv_first: float32 [1536, 4608], P(('fsdp', 'dp'))
- qkv_second: float32 [1536, 4608], P(('fsdp', 'dp')), may hold values from 327.68 to 1310.72
- out_weight: float32 [1536, 1536], P(('fsdp', 'dp')), may hold values from -0.15625 to 0.15625
- out_first: float32 [1536, 1536], P(('fsdp', 'dp'))
- out_second: float32 [1536, 1536], P(('fsdp', 'dp')), may hold values from 147.456 to 589.824
- gateup_weight: float32 [1536, 8192], P(('fsdp', 'dp')), may hold values from -0.15625 to 0.15625
- gateup_first: float32 [1536, 8192], P(('fsdp', 'dp'))
- gateup_second: float32 [1536, 8192], P(('fsdp', 'dp')), may hold values from 25.6 to 102.4
- down_weight: float32 [4096, 1536], P(('fsdp', 'dp')), may hold values from -0.09375 to 0.09375
- down_first: float32 [4096, 1536], P(('fsdp', 'dp'))
- down_second: float32 [4096, 1536], P(('fsdp', 'dp')), may hold values from 65.536 to 262.144
- norm_gains: float32 [2, 1536], P(None, ('fsdp', 'dp')), may hold values from 0.5 to 1.5
- gains_first: float32 [2, 1536], P(None, ('fsdp', 'dp'))
- gains_second: float32 [2, 1536], P(None, ('fsdp', 'dp')), as said below
- lambdas: float32 [4, 64], replicated, may hold values from -0.5 to 0.5
- lambdas_first: float32 [4, 64], replicated
- lambdas_second: float32 [4, 64], replicated, may hold values from 2457.6 to 9830.4
- head_gain: float32 [128], replicated, may hold values from 0.5 to 1.5
- head_first: float32 [128], replicated
- head_second: float32 [128], replicated, may hold values from 1638.4 to 6553.6
Outputs:
- layer_output: bfloat16 [8192, 1536], P(('fsdp', 'dp'))
- input_grad: float32 [8192, 1536], P(('fsdp', 'dp'))
- qkv_new: float32 [1536, 4608], P(('fsdp', 'dp'))
- qkv_first_new: float32 [1536, 4608], P(('fsdp', 'dp'))
- qkv_second_new: float32 [1536, 4608], P(('fsdp', 'dp'))
- out_new: float32 [1536, 1536], P(('fsdp', 'dp'))
- out_first_new: float32 [1536, 1536], P(('fsdp', 'dp'))
- out_second_new: float32 [1536, 1536], P(('fsdp', 'dp'))
- gateup_new: float32 [1536, 8192], P(('fsdp', 'dp'))
- gateup_first_new: float32 [1536, 8192], P(('fsdp', 'dp'))
- gateup_second_new: float32 [1536, 8192], P(('fsdp', 'dp'))
- down_new: float32 [4096, 1536], P(('fsdp', 'dp'))
- down_first_new: float32 [4096, 1536], P(('fsdp', 'dp'))
- down_second_new: float32 [4096, 1536], P(('fsdp', 'dp'))
- gains_new: float32 [2, 1536], P(None, ('fsdp', 'dp'))
- gains_first_new: float32 [2, 1536], P(None, ('fsdp', 'dp'))
- gains_second_new: float32 [2, 1536], P(None, ('fsdp', 'dp'))
- lambdas_new: float32 [4, 64], replicated
- lambdas_first_new: float32 [4, 64], replicated
- lambdas_second_new: float32 [4, 64], replicated
- head_new: float32 [128], replicated
- head_first_new: float32 [128], replicated
- head_second_new: float32 [128], replicated
The draws below stay inside these ranges and needn't reach their ends.
Inputs may be any that keep to these rules, and one draw needn't show every extreme that they name: `gains_second`: positive.
All inputs are finite; a program needn't handle non-finite values.
Results may differ from the reference program's by a relative error of at most 0.028.
Values may be sent and summed in bfloat16 or wider, within the bound.
No kernel may reach another device: no remote copies, remote signals or barrier semaphores. Data moves between devices by JAX's collectives and lax.ppermute only.
A program may use at most 384 MiB of HBM per device.

```python
import math
from functools import partial
import jax
import jax.numpy as jnp
from jax import lax

D = 1536
HEADS = 12
HDIM = 64
FF = 4096
TOK_DEV = 256
STEP = 10
HQ = 1536
TOKENS = 8192
DEVICES = 32


def moment_draw(key, shape, level):
    spread = level * math.sqrt(TOKENS) / 9.0
    return jnp.clip(jax.random.normal(key, shape, jnp.float32), -4.0, 4.0) * spread


def draw_needle(key, part):
    key = jax.random.fold_in(key, 11)
    position = jnp.arange(TOKENS, dtype=jnp.int32)
    ticket = jax.random.randint(key, (TOKENS,), 0, 4 * TOKENS, dtype=jnp.int32)
    return (ticket < TOKENS + 2 * position).astype(jnp.int32)


def draw_qkv_first(key, part):
    key = jax.random.fold_in(key, 1)
    return moment_draw(key, (D, 3 * HQ), 0.87)


def draw_out_first(key, part):
    key = jax.random.fold_in(key, 2)
    return moment_draw(key, (HQ, D), 0.6)


def draw_gateup_first(key, part):
    key = jax.random.fold_in(key, 3)
    return moment_draw(key, (D, 2 * FF), 0.25)


def draw_down_first(key, part):
    key = jax.random.fold_in(key, 4)
    return moment_draw(key, (FF, D), 0.4)


def draw_gains_first(key, part):
    key = jax.random.fold_in(key, 5)
    rows = jnp.array([[1.4], [0.58]], jnp.float32)
    return moment_draw(key, (2, D), 1.0) * rows


def draw_gains_second(key, part):
    key = jax.random.fold_in(key, 8)
    rows = jnp.array([[2.0], [0.35]], jnp.float32) * (0.0526 * TOKENS)
    factor = jnp.exp(jax.random.uniform(key, (2, D), jnp.float32, 0.0, math.log(4.0)))
    return rows * factor


def draw_lambdas_first(key, part):
    key = jax.random.fold_in(key, 6)
    return moment_draw(key, (4, HDIM), 2.25)


def draw_head_first(key, part):
    key = jax.random.fold_in(key, 7)
    return moment_draw(key, (2 * HDIM,), 2.0)


def levels(key, shape, pieces, least, top_value):
    loudness, own = 1.0, jax.random.fold_in(key, 6)
    for axis_at, blocks in pieces:
        heights = jnp.exp(jax.random.uniform(jax.random.fold_in(own, axis_at), (blocks,), jnp.float32, least / len(pieces), top_value / len(pieces)))
        loudness = loudness * jnp.repeat(heights, shape[axis_at] // blocks).reshape([-1 if axis == axis_at else 1 for axis in range(len(shape))])
    return loudness


def bell_draw(rng, dims, scale, limit, shards=(), held_as=jnp.bfloat16):
    gain = levels(rng, dims, shards, -0.22, 0.18) if shards else 1.0
    values = jax.random.normal(rng, dims, jnp.float32) * scale * gain
    return jnp.minimum(jnp.maximum(values, -limit), limit).astype(held_as)


def setup_inputs(seed: int = 0) -> dict:
    streams_of = jax.random.split(jax.random.key(seed), 25)
    return {
        "inputs": bell_draw(streams_of[0], (TOKENS, D), 1.0, 6.0, ((0, 32),)),
        "cotangent": bell_draw(streams_of[1], (TOKENS, D), 1.0, 6.0, ((0, 32),)),
        "needle": draw_needle(jax.random.fold_in(streams_of[24], 71), 0),
        "qkv_weight": bell_draw(streams_of[3], (D, 3 * HQ), D ** -0.5, 0.15625, ((0, 32),), jnp.float32),
        "qkv_first": draw_qkv_first(jax.random.fold_in(streams_of[24], 71), 0),
        "qkv_second": jnp.clip(jnp.exp(math.log(1310.72) - 1.3862944 * jax.random.uniform(streams_of[5], (D, 3 * HQ), jnp.float32) ** levels(streams_of[5], (D, 3 * HQ), ((0, 32),), -0.2, 0.2)), 327.68, 1310.72),
        "out_weight": bell_draw(streams_of[6], (HQ, D), HQ ** -0.5, 0.15625, ((0, 32),), jnp.float32),
        "out_first": draw_out_first(jax.random.fold_in(streams_of[24], 71), 0),
        "out_second": jnp.clip(jnp.exp(math.log(589.824) - 1.3862944 * jax.random.uniform(streams_of[8], (HQ, D), jnp.float32) ** levels(streams_of[8], (HQ, D), ((0, 32),), -0.2, 0.2)), 147.456, 589.824),
        "gateup_weight": bell_draw(streams_of[9], (D, 2 * FF), D ** -0.5, 0.15625, ((0, 32),), jnp.float32),
        "gateup_first": draw_gateup_first(jax.random.fold_in(streams_of[24], 71), 0),
        "gateup_second": jnp.clip(jnp.exp(math.log(102.4) - 1.3862944 * jax.random.uniform(streams_of[11], (D, 2 * FF), jnp.float32) ** levels(streams_of[11], (D, 2 * FF), ((0, 32),), -0.2, 0.2)), 25.6, 102.4),
        "down_weight": bell_draw(streams_of[12], (FF, D), FF ** -0.5, 0.09375, ((0, 32),), jnp.float32),
        "down_first": draw_down_first(jax.random.fold_in(streams_of[24], 71), 0),
        "down_second": jnp.clip(jnp.exp(math.log(262.144) - 1.3862944 * jax.random.uniform(streams_of[14], (FF, D), jnp.float32) ** levels(streams_of[14], (FF, D), ((0, 32),), -0.2, 0.2)), 65.536, 262.144),
        "norm_gains": jnp.clip(1.0 + 0.1 * jax.random.normal(streams_of[15], (2, D), jnp.float32), 0.5, 1.5),
        "gains_first": draw_gains_first(jax.random.fold_in(streams_of[24], 71), 0),
        "gains_second": draw_gains_second(jax.random.fold_in(streams_of[24], 71), 0),
        "lambdas": bell_draw(streams_of[18], (4, HDIM), 0.15, 0.5, (), jnp.float32),
        "lambdas_first": draw_lambdas_first(jax.random.fold_in(streams_of[24], 71), 0),
        "lambdas_second": jnp.clip(jnp.exp(jax.random.uniform(streams_of[20], (4, HDIM), jnp.float32, math.log(2457.6), math.log(9830.4))), 2457.6, 9830.4),
        "head_gain": jnp.clip(1.0 + 0.1 * jax.random.normal(streams_of[21], (2 * HDIM,), jnp.float32), 0.5, 1.5),
        "head_first": draw_head_first(jax.random.fold_in(streams_of[24], 71), 0),
        "head_second": jnp.clip(jnp.exp(jax.random.uniform(streams_of[23], (2 * HDIM,), jnp.float32, math.log(1638.4), math.log(6553.6))), 1638.4, 6553.6),
    }


NORM_EPSILON = 1e-05
LAMBDA_INIT = 0.2
BETA_FIRST = 0.9
BETA_SECOND = 0.95
ADAM_EPSILON = 1e-08
WEIGHT_DECAY = 0.1
RATE_MATRIX = 0.02
RATE_GAIN = 0.5
RATE_LAMBDA = 0.15
MASKED = -1000000000.0
HIGHEST = lax.Precision.HIGHEST

@jax.custom_vjp
def low(v):
    return lax.optimization_barrier(v.astype(jnp.bfloat16)).astype(jnp.float32)

@jax.custom_vjp
def low_back(v):
    return v

def low_keep(v):
    return (low(v), None)

def low_pass(kept, grad):
    return (grad,)

def back_keep(v):
    return (v, None)

def back_low(kept, grad):
    return (low(grad),)
low.defvjp(low_keep, low_pass)
low_back.defvjp(back_keep, back_low)

def rms_scale(values):
    return lax.rsqrt(lax.optimization_barrier(jnp.mean(values * values, axis=-1, keepdims=True)) + NORM_EPSILON)

def sequence_forward(weights, activations):
    qkv_full, out_full, gateup_full, down_full, gains_full, lambdas, head_gain = weights
    length = activations.shape[0]
    inner_width = HEADS * 2 * HDIM
    normed_one = low(activations * rms_scale(activations) * gains_full[0])
    projected = low_back(low(jnp.dot(normed_one, qkv_full, precision=HIGHEST)))
    queries = projected[:, :inner_width].reshape(length, HEADS, 2, HDIM)
    key_rows = projected[:, inner_width:2 * inner_width].reshape(length, HEADS, 2, HDIM)
    value_rows = projected[:, 2 * inner_width:].reshape(length, HEADS, 2 * HDIM)
    mixing = jnp.exp(jnp.sum(lambdas[0] * lambdas[1])) - jnp.exp(jnp.sum(lambdas[2] * lambdas[3])) + LAMBDA_INIT
    position = jnp.arange(length)
    allowed = position[:, None] >= position[None, :]
    scores = jnp.einsum('qhcd,khcd->hcqk', queries, key_rows, precision=HIGHEST) * HDIM ** (-0.5)
    scores = low_back(scores)
    scores = jnp.where(allowed, scores, MASKED)
    probabilities = jax.nn.softmax(scores, axis=-1)
    mixed_rows = low(probabilities[:, 0] - mixing * probabilities[:, 1])
    attended = low_back(jnp.einsum('hqk,khe->qhe', mixed_rows, value_rows, precision=HIGHEST))
    head_normed = attended * rms_scale(attended) * head_gain * (1.0 - LAMBDA_INIT)
    merged = low(head_normed.reshape(length, inner_width))
    residual = activations + low_back(jnp.dot(merged, out_full, precision=HIGHEST))
    normed_two = low(residual * rms_scale(residual) * gains_full[1])
    gate_up = low_back(jnp.dot(normed_two, gateup_full, precision=HIGHEST))
    hidden = low(jax.nn.silu(gate_up[:, :FF]) * gate_up[:, FF:])
    return residual + low_back(jnp.dot(hidden, down_full, precision=HIGHEST))

def layer_forward(params, activations):
    qkv_w, out_w, gateup_w, down_w, gains_w, lambdas, head_gain = params
    weights = (low(qkv_w), low(out_w), low(gateup_w), low(down_w), low(gains_w), lambdas, head_gain)
    group = min(DEVICES, max(1, 4096 // TOK_DEV))
    stacked = activations.reshape(DEVICES // group, group, TOK_DEV, D)

    def run_group(state_in, group_rows):
        return (state_in, jax.vmap(partial(sequence_forward, weights))(group_rows))
    state_out, outputs = lax.scan(jax.checkpoint(run_group), jnp.zeros((), jnp.float32), stacked)
    return outputs.reshape(TOKENS, D)

def adam_update(weight, first, second, grad, rate, decay):
    first_new = BETA_FIRST * first + (1.0 - BETA_FIRST) * grad
    second_new = BETA_SECOND * second + (1.0 - BETA_SECOND) * grad * grad
    corrected_first = first_new / (1.0 - BETA_FIRST ** STEP)
    corrected_second = second_new / (1.0 - BETA_SECOND ** STEP)
    weight_new = weight - rate * (corrected_first / (jnp.sqrt(corrected_second) + ADAM_EPSILON) + decay * weight)
    return (weight_new, first_new, second_new)

def reference(inputs, cotangent, needle, qkv_weight, qkv_first, qkv_second, out_weight, out_first, out_second, gateup_weight, gateup_first, gateup_second, down_weight, down_first, down_second, norm_gains, gains_first, gains_second, lambdas, lambdas_first, lambdas_second, head_gain, head_first, head_second):
    params = (qkv_weight, out_weight, gateup_weight, down_weight, norm_gains, lambdas, head_gain)
    output, pullback = jax.vjp(layer_forward, params, inputs.astype(jnp.float32))
    weighted = cotangent.astype(jnp.float32) * needle.astype(jnp.float32)[:, None]
    grads, input_grad = pullback(weighted)
    qkv_grad, out_grad, gateup_grad, down_grad, gains_grad, lambdas_grad, head_grad = grads
    qkv_res = adam_update(qkv_weight, qkv_first, qkv_second, qkv_grad, RATE_MATRIX, WEIGHT_DECAY)
    out_res = adam_update(out_weight, out_first, out_second, out_grad, RATE_MATRIX, WEIGHT_DECAY)
    gateup_res = adam_update(gateup_weight, gateup_first, gateup_second, gateup_grad, RATE_MATRIX, WEIGHT_DECAY)
    down_res = adam_update(down_weight, down_first, down_second, down_grad, RATE_MATRIX, WEIGHT_DECAY)
    gains_res = adam_update(norm_gains, gains_first, gains_second, gains_grad, RATE_GAIN, 0.0)
    lambdas_res = adam_update(lambdas, lambdas_first, lambdas_second, lambdas_grad, RATE_LAMBDA, 0.0)
    head_res = adam_update(head_gain, head_first, head_second, head_grad, RATE_GAIN, 0.0)
    return (output.astype(jnp.bfloat16), input_grad, qkv_res[0], qkv_res[1], qkv_res[2], out_res[0], out_res[1], out_res[2], gateup_res[0], gateup_res[1], gateup_res[2], down_res[0], down_res[1], down_res[2], gains_res[0], gains_res[1], gains_res[2], lambdas_res[0], lambdas_res[1], lambdas_res[2], head_res[0], head_res[1], head_res[2])
```

```python
import functools

import jax
import jax.numpy as jnp
from jax import lax
from jax.experimental import pallas as pl
from jax.experimental.pallas import tpu as pltpu
from jax.sharding import Mesh
from jax.sharding import PartitionSpec as P

HEADS = 12
HDIM = 64
HEAD = 2 * HDIM
FF = 4096
STEP = 10
PLANE = 4
LOCAL_HEADS = HEADS // PLANE
LOCAL_FF = FF // PLANE
LOCAL_Q = LOCAL_HEADS * HEAD

NORM_EPSILON = 1e-05
LAMBDA_INIT = 0.2
FACTOR = 1.0 - LAMBDA_INIT
BETA_FIRST = 0.9
BETA_SECOND = 0.95
ADAM_EPSILON = 1e-08
WEIGHT_DECAY = 0.1
RATE_MATRIX = 0.02
RATE_GAIN = 0.5
RATE_LAMBDA = 0.15
MASKED = -1000000000.0
SCALE = HDIM ** (-0.5)

BF16 = jnp.bfloat16
F32 = jnp.float32
VMEM_LIMIT = 48 * 1024 * 1024
AXES = ("j", "c", "dp")


def rms_scale(values):
    return lax.rsqrt(jnp.mean(values * values, axis=-1, keepdims=True) + NORM_EPSILON)


def mm(left, right):
    return lax.dot_general(left, right, (((1,), (0,)), ((), ())), preferred_element_type=F32)


def mm_nt(left, right):
    return lax.dot_general(left, right, (((1,), (1,)), ((), ())), preferred_element_type=F32)


def mm_tn(left, right):
    return lax.dot_general(left, right, (((0,), (0,)), ((), ())), preferred_element_type=F32)


def softmax_pair(q, k, rows):
    first = lax.broadcasted_iota(jnp.int32, (rows, HEAD), 1) < HDIM
    allowed = lax.broadcasted_iota(jnp.int32, (rows, rows), 0) >= lax.broadcasted_iota(
        jnp.int32, (rows, rows), 1
    )
    zero = jnp.zeros_like(q)
    result = []
    for half in (jnp.where(first, q, zero), jnp.where(first, zero, q)):
        scores = jnp.where(allowed, mm_nt(half, k) * SCALE, MASKED)
        terms = jnp.exp(scores - jnp.max(scores, axis=-1, keepdims=True))
        result.append(terms * (1.0 / jnp.sum(terms, axis=-1, keepdims=True)))
    return result


def attend_kernel(x_ref, gain_ref, wq_ref, wo_ref, lam_ref, hg_ref, n_ref, p_ref, g_ref, o_ref):
    rows = x_ref.shape[0]
    x = x_ref[...].astype(F32)
    n_ref[...] = (x * rms_scale(x) * gain_ref[...]).astype(BF16)
    for part in range(3):
        cols = pl.ds(part * LOCAL_Q, LOCAL_Q)
        p_ref[:, cols] = mm(n_ref[...], wq_ref[:, cols]).astype(BF16)
    lam = lam_ref[0, 0]
    for head in range(LOCAL_HEADS):
        q, k, v = (
            p_ref[:, pl.ds(part * LOCAL_Q + head * HEAD, HEAD)] for part in range(3)
        )
        a1, a2 = softmax_pair(q, k, rows)
        mixed = (a1 - lam * a2).astype(BF16)
        out = mm(mixed, v)
        g_ref[:, pl.ds(head * HEAD, HEAD)] = (
            out * rms_scale(out) * hg_ref[...] * FACTOR
        ).astype(BF16)
    o_ref[...] = mm(g_ref[...], wo_ref[...]).astype(BF16)


def ffn_kernel(count, *refs):
    n_refs, dy_refs, (wgu_ref, wd_ref) = refs[:count], refs[count : 2 * count], refs[2 * count :][:2]
    outs, (hidden_ref, grad_ref) = refs[2 * count + 2 : -2], refs[-2:]
    length = n_refs[0].shape[0]
    normed = jnp.concatenate([ref[...] for ref in n_refs], axis=0)
    gate = mm(normed, wgu_ref[:, :LOCAL_FF])
    up = mm(normed, wgu_ref[:, LOCAL_FF:])
    dh = mm_nt(jnp.concatenate([ref[...] for ref in dy_refs], axis=0), wd_ref[...])
    sig = 0.5 * jnp.tanh(0.5 * gate) + 0.5
    silu = gate * sig
    hidden_ref[...] = (silu * up).astype(BF16)
    grad_ref[:, :LOCAL_FF] = (dh * up * (sig + silu * (1.0 - sig))).astype(BF16)
    grad_ref[:, LOCAL_FF:] = (dh * silu).astype(BF16)
    out = mm(hidden_ref[...], wd_ref[...]).astype(BF16)
    back = mm_nt(grad_ref[...], wgu_ref[...]).astype(BF16)
    for i in range(count):
        at = slice(i * length, (i + 1) * length)
        y_ref, dn_ref, h_ref, du_ref = outs[4 * i : 4 * i + 4]
        y_ref[...] = out[at]
        dn_ref[...] = back[at]
        h_ref[...] = hidden_ref[at, :]
        du_ref[...] = grad_ref[at, :]


def attend_back_kernel(
    dh_ref, p_ref, wq_ref, wo_ref, lam_ref, hg_ref, dp_ref, dn_ref, stat_ref, dg_ref
):
    rows = dh_ref.shape[0]
    dg_ref[...] = mm_nt(dh_ref[...], wo_ref[...])
    lam = lam_ref[0, 0]
    hg = hg_ref[...]
    first = lax.broadcasted_iota(jnp.int32, (rows, HEAD), 1) < HDIM
    grad_hg = jnp.zeros((1, HEAD), F32)
    grad_lam = jnp.zeros((1, 1), F32)
    for head in range(LOCAL_HEADS):
        q, k, v = (
            p_ref[:, pl.ds(part * LOCAL_Q + head * HEAD, HEAD)] for part in range(3)
        )
        a1, a2 = softmax_pair(q, k, rows)
        mixed = (a1 - lam * a2).astype(BF16)
        out = mm(mixed, v)
        scale = rms_scale(out)
        unit = out * scale
        dg = dg_ref[:, pl.ds(head * HEAD, HEAD)]
        grad_hg = grad_hg + FACTOR * jnp.sum(dg * unit, axis=0, keepdims=True)
        u = dg * hg * FACTOR
        dout = (scale * (u - unit * jnp.mean(u * unit, axis=-1, keepdims=True))).astype(BF16)
        dv = mm_tn(mixed, dout)
        dm = mm_nt(dout, v)
        dot1 = jnp.sum(dm * a1, axis=-1, keepdims=True)
        dot2 = jnp.sum(dm * a2, axis=-1, keepdims=True)
        grad_lam = grad_lam - jnp.sum(dot2, axis=0, keepdims=True)
        ds1 = (a1 * (dm - dot1)).astype(BF16)
        ds2 = (-lam * a2 * (dm - dot2)).astype(BF16)
        dq = jnp.where(first, mm(ds1, k), mm(ds2, k)) * SCALE
        dk = jnp.where(first, mm_tn(ds1, q), mm_tn(ds2, q)) * SCALE
        for part, value in enumerate((dq, dk, dv)):
            dp_ref[:, pl.ds(part * LOCAL_Q + head * HEAD, HEAD)] = value.astype(BF16)
    stat_ref[0:1, :] = grad_hg
    stat_ref[1:2, :] = jnp.broadcast_to(grad_lam, (1, HEAD))
    dn_ref[...] = mm_nt(dp_ref[...], wq_ref[:, : 3 * LOCAL_Q]).astype(BF16)


def split_kernel(pos_ref, qkv_ref, gain_ref, gateup_ref, *outs):
    rows = qkv_ref.shape[0]
    gains = jnp.concatenate([gain_ref[...], jnp.zeros((HEAD - 2, rows), F32)], axis=0).T
    for r in range(PLANE):
        q = pos_ref[0] ^ r
        start = 0
        for w_ref, parts in ((qkv_ref, 3), (gateup_ref, 2)):
            width = w_ref.shape[1] // parts
            quarter = width // PLANE
            for part in range(parts):
                cols = pl.ds(pl.multiple_of(part * width + q * quarter, HEAD), quarter)
                outs[r][:, start : start + quarter] = w_ref[:, cols].astype(BF16)
                start += quarter
            if parts == 3:
                outs[r][:, start : start + HEAD] = gains.astype(BF16)
                start += HEAD


def reorder_kernel(in_ref, out_ref, sem):
    count = in_ref.shape[0]
    copies = [
        pltpu.make_async_copy(in_ref.at[k], out_ref.at[:, k], sem.at[k]) for k in range(count)
    ]
    for copy in copies:
        copy.start()
    for copy in copies:
        copy.wait()


def down_blocks(rows):
    tall, block = rows * 3 // 4, 512
    cuts = sorted({*range(0, 3 * rows + 1, rows), *range(0, 3 * rows + 1, tall)})
    for at, stop in zip(cuts, cuts[1:]):
        yield at % rows, at // rows * block, at % tall, at // tall * block, stop - at


def message_kernel(slot_ref, *refs):
    pieces, (weight_ref, down_ref, out_ref, second_ref, sem) = refs[:PLANE], refs[PLANE:]
    rows, columns = pieces[0].shape
    wide = columns - second_ref.shape[1]
    copies = []
    for r in range(PLANE):
        cols = pl.ds(pl.multiple_of(slot_ref[r] * wide, HEAD), wide)
        copies.append(
            pltpu.make_async_copy(pieces[r].at[:, pl.ds(0, wide)], out_ref.at[:, cols], sem.at[r, 0])
        )
        copies.append(
            pltpu.make_async_copy(
                pieces[r].at[:, pl.ds(wide, second_ref.shape[1])],
                second_ref.at[pl.ds(pl.multiple_of(slot_ref[r] * rows, 16), rows)],
                sem.at[r, 1],
            )
        )
    for copy in copies:
        copy.start()
    out_ref[:, PLANE * wide :] = weight_ref[...].astype(BF16)
    for row, col, to_row, to_col, count in down_blocks(down_ref.shape[0]):
        second_ref[pl.ds(PLANE * rows + to_row, count), pl.ds(to_col, 512)] = down_ref[
            row : row + count, col : col + 512
        ].astype(BF16)
    for copy in copies:
        copy.wait()


def message_plain_kernel(slot_ref, *refs):
    pieces, (weight_ref, out_ref, gateup_ref, sem) = refs[:PLANE], refs[PLANE:]
    wide = pieces[0].shape[1] - gateup_ref.shape[2]
    copies = []
    for r in range(PLANE):
        cols = pl.ds(pl.multiple_of(slot_ref[r] * wide, HEAD), wide)
        copies.append(
            pltpu.make_async_copy(pieces[r].at[:, pl.ds(0, wide)], out_ref.at[:, cols], sem.at[r, 0])
        )
        copies.append(
            pltpu.make_async_copy(
                pieces[r].at[:, pl.ds(wide, gateup_ref.shape[2])], gateup_ref.at[slot_ref[r]], sem.at[r, 1]
            )
        )
    for copy in copies:
        copy.start()
    out_ref[:, PLANE * wide :] = weight_ref[...].astype(BF16)
    for copy in copies:
        copy.wait()


def place_second_kernel(in_ref, blocks_ref, gateup_ref, down_ref, sem):
    rows, tall = gateup_ref.shape[2], down_ref.shape[1]
    copies = []
    for k in range(in_ref.shape[0]):
        copies.append((blocks_ref.at[k, pl.ds(0, PLANE)], gateup_ref.at[:, k]))
        for row, col, to_row, to_col, count in down_blocks(tall):
            copies.append(
                (
                    in_ref.at[k, pl.ds(PLANE * rows + to_row, count), pl.ds(to_col, 512)],
                    down_ref.at[k, pl.ds(row, count), pl.ds(col, 512)],
                )
            )
    copies = [pltpu.make_async_copy(a, b, sem.at[i]) for i, (a, b) in enumerate(copies)]
    for copy in copies:
        copy.start()
    for copy in copies:
        copy.wait()


def place_first_kernel(in_ref, qkv_ref, out_ref, gain_ref, sem):
    count, (rows, wide) = in_ref.shape[0], qkv_ref.shape[2:]
    copies = []
    for k in range(count):
        for j in range(PLANE):
            copies.append((in_ref.at[k, :, pl.ds(j * wide, wide)], qkv_ref.at[j, k]))
        copies.append((in_ref.at[k, :, pl.ds(PLANE * wide, out_ref.shape[2])], out_ref.at[k]))
    copies = [pltpu.make_async_copy(a, b, sem.at[i]) for i, (a, b) in enumerate(copies)]
    for copy in copies:
        copy.start()
    for copy in copies:
        copy.wait()
    columns = qkv_ref[:, :, :, 3 * LOCAL_Q :].astype(F32).reshape(PLANE * count * rows, HEAD)
    gain_ref[...] = columns.T[:8]


def weight_grad_kernel(m, pos_ref, *refs):
    lefts, rights, outs = refs[:PLANE], refs[PLANE : 2 * PLANE], refs[2 * PLANE : 2 * PLANE + m]
    left, right, total, sem = refs[2 * PLANE + m :]
    length = lefts[0].shape[0]
    copies = []
    for r in range(PLANE):
        for i, (src, dst) in enumerate(((lefts[r], left), (rights[r], right))):
            copies.append(
                pltpu.make_async_copy(
                    src, dst.at[pl.ds(r * length, length)], sem.at[2 * r + i]
                )
            )
            copies[-1].start()
    for copy in copies:
        copy.wait()
    rows, columns = total.shape
    share = rows // m
    for lead in range(outs[0].shape[0]):
        value = mm_tn(left[:, lead * rows : (lead + 1) * rows], right[...])
        if m == 2:
            top, low = value[:share].astype(BF16), value[share:].astype(BF16)
            outs[0][lead] = jnp.where(pos_ref[1] == 0, top, low)
            outs[1][lead] = jnp.where(pos_ref[1] == 0, low, top)
        else:
            total[...] = value
            for k in range(m):
                start = pl.multiple_of(((pos_ref[1] + k) % m) * share, 8)
                outs[k][lead] = total[pl.ds(start, share), :].astype(BF16)


def chunk_second_kernel(m, *refs):
    gateup, down, out = refs[:m], refs[m : 2 * m], refs[2 * m]
    d = out.shape[0]
    rows, tall = gateup[0].shape[1] // d, down[0].shape[1] // d
    for z in range(d):
        for j in range(PLANE):
            value = add_up([term[j, z * rows : (z + 1) * rows, :] for term in gateup])
            out[z, j * rows : (j + 1) * rows, :] = value.astype(BF16)
        value = add_up([term[0, z * tall : (z + 1) * tall, :] for term in down]).astype(BF16)
        for row, col, to_row, to_col, count in down_blocks(tall):
            out[z, pl.ds(PLANE * rows + to_row, count), pl.ds(to_col, 512)] = value[
                row : row + count, col : col + 512
            ]


def chunk_first_kernel(m, *refs):
    qkv, out_terms, out = refs[:m], refs[m : 2 * m], refs[2 * m]
    d, rows, _ = out.shape
    wide = qkv[0].shape[2]
    for z in range(d):
        for j in range(PLANE + 1):
            terms, lead = (qkv, j) if j < PLANE else (out_terms, 0)
            value = add_up([term[lead, z * rows : (z + 1) * rows, :] for term in terms])
            out[z, :, j * wide : j * wide + value.shape[1]] = value.astype(BF16)


def owner_first_kernel(pos_ref, in_ref, *outs):
    *outs, out_ref = outs
    wide = outs[0].shape[1]
    for r in range(PLANE):
        outs[r][...] = in_ref[:, pl.ds(pl.multiple_of((pos_ref[0] ^ r) * wide, HEAD), wide)]
    out_ref[...] = in_ref[:, PLANE * wide :].astype(F32)


def owner_second_kernel(pos_ref, in_ref, *outs):
    *outs, down_ref = outs
    rows, tall = outs[0].shape[0], down_ref.shape[0]
    for r in range(PLANE):
        outs[r][...] = in_ref[pl.ds(pl.multiple_of((pos_ref[0] ^ r) * rows, 16), rows), :]
    for row, col, to_row, to_col, count in down_blocks(tall):
        down_ref[row : row + count, col : col + 512] = in_ref[
            pl.ds(PLANE * rows + to_row, count), pl.ds(to_col, 512)
        ].astype(F32)


def adam_columns_kernel(parts, width, pos_ref, *refs):
    pieces, (w_ref, f_ref, s_ref, wn_ref, fn_ref, sn_ref, dot_ref) = refs[:PLANE], refs[PLANE:]
    quarter = width // PLANE
    dot = jnp.zeros((w_ref.shape[0], 1), F32)
    for r in range(PLANE):
        q = pos_ref[0] ^ r
        for part in range(parts):
            cols = pl.ds(pl.multiple_of(part * width + q * quarter, HEAD), quarter)
            grad = pieces[r][:, part * quarter : (part + 1) * quarter].astype(F32)
            weight = w_ref[:, cols]
            dot = dot + jnp.sum(weight.astype(BF16).astype(F32) * grad, axis=1, keepdims=True)
            wn_ref[:, cols], fn_ref[:, cols], sn_ref[:, cols] = adam_update(
                weight, f_ref[:, cols], s_ref[:, cols], grad, RATE_MATRIX, WEIGHT_DECAY
            )
    dot_ref[...] = jnp.broadcast_to(dot, (dot.shape[0], HEAD)).T[:8]


ANY = pl.BlockSpec(memory_space=pl.ANY)
VMEM = pl.BlockSpec(memory_space=pltpu.VMEM)
SMEM = pl.BlockSpec(memory_space=pltpu.SMEM)


def call(kernel, outs, operands, scratch=(), flops=0, specs=None, out_spec=VMEM):
    size = sum(a.size * a.dtype.itemsize for a in operands) + sum(
        o.size * o.dtype.itemsize for o in outs
    )
    return pl.pallas_call(
        kernel,
        out_shape=tuple(outs),
        in_specs=specs or [VMEM] * len(operands),
        out_specs=(out_spec,) * len(outs),
        scratch_shapes=list(scratch),
        compiler_params=pltpu.CompilerParams(vmem_limit_bytes=VMEM_LIMIT),
        cost_estimate=pl.CostEstimate(flops=0, bytes_accessed=0, transcendentals=0),
    )(*operands)


def shaped(*shape, dtype=BF16):
    return jax.ShapeDtypeStruct(shape, dtype)


def tie(value, *after):
    return lax.optimization_barrier((value, *after))[0]


class Group:
    def __init__(self, m, d):
        self.m, self.d = m, d
        self.j, self.c, self.z = (lax.axis_index(axis) for axis in AXES)
        self.pos = jnp.stack([self.j, self.c, self.z]).astype(jnp.int32)

    def plane(self, value, r):
        return lax.ppermute(value, "j", [(i, i ^ r) for i in range(PLANE)])

    def core(self, value, k):
        return lax.ppermute(value, "c", [(i, (i + k) % self.m) for i in range(self.m)])

    def everyone(self, value):
        n, step = PLANE * self.m * self.d, 1
        while step < n:
            value = value + lax.ppermute(value, AXES, [(i, i ^ step) for i in range(n)])
            step *= 2
        return value


def plane_near(grp, own):
    return [own, grp.plane(own, 1), grp.plane(own, 2)]


def plane_far(grp, near, *after):
    own, one, two = near
    half = own.shape[0] // 2
    if after:
        one, two = tie(one, *after), tie(two, *after)
    three = jnp.concatenate([grp.plane(one[:half], 2), grp.plane(two[half:], 1)], axis=0)
    return [own, one, two, three]


def plane_gather(grp, own):
    return plane_far(grp, plane_near(grp, own))


def plane_send(grp, parts):
    return [parts[0]] + [grp.plane(parts[r], r) for r in range(1, PLANE)]


def plane_scatter_first(grp, parts, axis):
    return grp.plane(jnp.concatenate([parts[axis], parts[3]], axis=0), axis)


def plane_scatter_second(grp, parts, axis, got):
    half = parts[0].shape[0]
    sent = add_up([parts[3 - axis], got[half:]]).astype(BF16)
    return [parts[0], got[:half], grp.plane(sent, 3 - axis)], sent


def add_up(terms):
    return sum(term.astype(F32) for term in terms)


def exchange(grp, pieces):
    return [pieces[0]] + [grp.plane(pieces[r], r) for r in range(1, PLANE)]


def core_terms(grp, halves):
    return [halves[0]] + [grp.core(halves[k], k) for k in range(1, grp.m)]


def spread(grp, kernel, shape, wide, tall):
    message = call(
        functools.partial(kernel, grp.m),
        (shaped(grp.d, *shape),),
        (*core_terms(grp, wide), *core_terms(grp, tall)),
    )[0]
    return message, lax.psum_scatter(message, "dp", scatter_dimension=0, tiled=False)


def owner(grp, kernel, message, piece, rest):
    *pieces, out = call(
        kernel,
        (shaped(*piece),) * PLANE + (shaped(*rest, dtype=F32),),
        (grp.pos, message),
        specs=[SMEM, VMEM],
    )
    return pieces, out


def owner_plain(grp, halves):
    d, m = grp.d, grp.m
    full = jnp.stack([lax.dynamic_index_in_dim(jnp.stack(halves), (k - grp.c) % m, 0, False) for k in range(m)])
    lead, rows, columns = halves[0].shape
    full = full.reshape(m, lead, d, rows // d, columns).transpose(0, 2, 1, 3, 4)
    full = full.reshape(m * d, lead, rows // d, columns)
    return lax.psum_scatter(full, ("c", "dp"), scatter_dimension=0, tiled=False).astype(F32)


def weight_grad(grp, lefts, rights, lead):
    length, rows = lefts[0].shape
    columns = rights[0].shape[1]
    share = rows // lead // grp.m
    return call(
        functools.partial(weight_grad_kernel, grp.m),
        (shaped(lead, share, columns),) * grp.m,
        (grp.pos, *lefts, *rights),
        scratch=(
            pltpu.VMEM((PLANE * length, rows), BF16),
            pltpu.VMEM((PLANE * length, columns), BF16),
            pltpu.VMEM((rows // lead, columns), F32),
            pltpu.SemaphoreType.DMA((2 * PLANE,)),
        ),
        specs=[SMEM] + [ANY] * (2 * PLANE),
        flops=2 * PLANE * length * rows * columns,
    )


def adam_columns(grp, pieces, weight, first, second, parts):
    rows, columns = weight.shape
    return call(
        functools.partial(adam_columns_kernel, parts, columns // parts),
        (shaped(rows, columns, dtype=F32),) * 3 + (shaped(8, rows, dtype=F32),),
        (grp.pos, *pieces, weight, first, second),
        specs=[SMEM] + [VMEM] * (PLANE + 3),
    )


def norm_back(grad_normed, values, gain):
    scale_rows = rms_scale(values)
    scaled = grad_normed * gain
    unit_rows = values * scale_rows
    return scale_rows * (
        scaled - unit_rows * jnp.mean(scaled * unit_rows, axis=-1, keepdims=True)
    )


def adam_update(weight, first, second, grad, rate, decay):
    first_new = BETA_FIRST * first + (1.0 - BETA_FIRST) * grad
    second_new = BETA_SECOND * second + (1.0 - BETA_SECOND) * grad * grad
    corrected_first = first_new / (1.0 - BETA_FIRST**STEP)
    corrected_second = second_new / (1.0 - BETA_SECOND**STEP)
    weight_new = weight - rate * (
        corrected_first / (jnp.sqrt(corrected_second) + ADAM_EPSILON) + decay * weight
    )
    return (weight_new, first_new, second_new)


def per_device(
    members,
    d,
    inputs,
    cotangent,
    needle,
    qkv_weight,
    qkv_first,
    qkv_second,
    out_weight,
    out_first,
    out_second,
    gateup_weight,
    gateup_first,
    gateup_second,
    down_weight,
    down_first,
    down_second,
    norm_gains,
    gains_first,
    gains_second,
    lambdas,
    lambdas_first,
    lambdas_second,
    head_gain,
    head_first,
    head_second,
):
    grp = Group(members, d)
    length, width = inputs.shape
    rows = qkv_weight.shape[0]
    struct = jax.ShapeDtypeStruct

    gains_low = norm_gains.astype(BF16)
    plane_slots = jnp.stack([grp.j ^ r for r in range(PLANE)]).astype(jnp.int32)
    wide = 3 * LOCAL_Q + HEAD
    quarters = call(
        split_kernel,
        (shaped(rows, wide + 2 * LOCAL_FF),) * PLANE,
        (grp.pos, qkv_weight, norm_gains, gateup_weight),
        specs=[SMEM] + [VMEM] * 3,
    )
    tuned = rows % 16 == 0
    count = members * d
    everywhere = functools.partial(lax.all_gather, axis_name=("c", "dp"), axis=0, tiled=False)
    exchanged = exchange(grp, quarters)
    if tuned:
        first_message, second_message = call(
            message_kernel,
            (
                shaped(rows, PLANE * wide + width),
                shaped(PLANE * rows + down_weight.shape[0] * 3 // 4, 2 * LOCAL_FF),
            ),
            (plane_slots, *exchanged, out_weight, down_weight),
            scratch=(pltpu.SemaphoreType.DMA((PLANE, 2)),),
            specs=[SMEM] + [ANY] * PLANE + [VMEM] * 2,
        )
    else:
        first_message, second_message = call(
            message_plain_kernel,
            (shaped(rows, PLANE * wide + width), shaped(PLANE, rows, 2 * LOCAL_FF)),
            (plane_slots, *exchanged, out_weight),
            scratch=(pltpu.SemaphoreType.DMA((PLANE, 2)),),
            specs=[SMEM] + [ANY] * PLANE + [VMEM],
        )
    x_blocks = plane_gather(grp, tie(inputs, first_message))
    first_all = everywhere(first_message)
    second_all = everywhere(tie(second_message, *x_blocks[1:3]))
    grad_out = cotangent.astype(F32) * needle.astype(F32)[:, None]
    dy_near = plane_near(grp, tie(grad_out, x_blocks[3]).astype(BF16))
    first_all = tie(first_all, x_blocks[3], *dy_near[1:])
    qkv_full, out_full, gains_full = call(
        place_first_kernel,
        (
            shaped(PLANE, count, rows, wide),
            shaped(count, rows, width),
            shaped(8, width, dtype=F32),
        ),
        (first_all,),
        scratch=(pltpu.SemaphoreType.DMA((count * (PLANE + 1),)),),
        specs=[ANY],
    )
    qkv_full, out_full = qkv_full.reshape(width, wide), out_full.reshape(LOCAL_Q, width)
    gain_one, gain_two = gains_full[0:1], gains_full[1:2]
    first_term = jnp.exp(jnp.sum(lambdas[0] * lambdas[1]))
    second_term = jnp.exp(jnp.sum(lambdas[2] * lambdas[3]))
    mixing = first_term - second_term + LAMBDA_INIT
    lam = jnp.broadcast_to(mixing, (1, HEAD))
    hg = head_gain.reshape(1, HEAD)

    activations = inputs.astype(F32)
    order = (3, 1, 2, 0)
    normed_one, projected, merged, parts = ([None] * PLANE for _ in range(4))
    for r in order:
        normed_one[r], projected[r], merged[r], parts[r] = call(
            attend_kernel,
            (
                struct((length, width), BF16),
                struct((length, 3 * LOCAL_Q), BF16),
                struct((length, LOCAL_Q), BF16),
                struct((length, width), BF16),
            ),
            (x_blocks[r], gain_one, qkv_full, out_full, lam, hg),
            flops=2 * length * width * 4 * LOCAL_Q,
        )
    dy_blocks = plane_far(grp, dy_near, parts[0])
    residual = activations + add_up(plane_send(grp, parts))
    normed_two = (residual * rms_scale(residual) * gain_two).astype(BF16)

    n2_near = plane_near(grp, normed_two)
    n2_blocks = plane_far(grp, n2_near)
    second_all = tie(second_all, n2_near[1], n2_near[2])
    if tuned:
        gateup_full, down_full = call(
            place_second_kernel,
            (
                shaped(PLANE, count, rows, 2 * LOCAL_FF),
                shaped(count, *down_weight.shape),
            ),
            (second_all, second_all.reshape(count, -1, rows, 2 * LOCAL_FF)),
            scratch=(pltpu.SemaphoreType.DMA((count * 7,)),),
            specs=[ANY] * 2,
        )
        gateup_full, down_full = gateup_full.reshape(width, -1), down_full.reshape(-1, width)
    else:
        gateup_full = second_all.transpose(1, 0, 2, 3).reshape(width, -1)
        down_full = everywhere(down_weight.astype(BF16)).reshape(-1, width)
    y_parts, dn2_parts, hidden, grad_gate_up, dn2_terms = ([None] * PLANE for _ in range(5))
    after = ()
    for pair in ((3, 1), (2, 0)):
        results = call(
            functools.partial(ffn_kernel, 2),
            (
                shaped(length, width),
                shaped(length, width),
                shaped(length, LOCAL_FF),
                shaped(length, 2 * LOCAL_FF),
            )
            * 2,
            (
                *(tie(n2_blocks[r], *after) if after else n2_blocks[r] for r in pair),
                *(dy_blocks[r] for r in pair),
                gateup_full,
                down_full,
            ),
            scratch=(
                pltpu.VMEM((2 * length, LOCAL_FF), BF16),
                pltpu.VMEM((2 * length, 2 * LOCAL_FF), BF16),
            ),
        )
        for i, r in enumerate(pair):
            y_parts[r], dn2_parts[r], hidden[r], grad_gate_up[r] = results[4 * i : 4 * i + 4]
            dn2_terms[r] = grp.plane(dn2_parts[r], r) if r else dn2_parts[r]
        after = (y_parts[1],)
    grad_residual = grad_out + norm_back(add_up(dn2_terms), residual, gain_two)
    gateup_halves = weight_grad(
        grp, [tie(n2_blocks[0], y_parts[0], dn2_terms[3]), *n2_blocks[1:]], grad_gate_up, PLANE
    )
    down_halves = weight_grad(grp, [tie(hidden[0], gateup_halves[0], *dn2_terms[1:3]), *hidden[1:]], dy_blocks, 1)
    if tuned:
        mark, second_sum = spread(
            grp,
            chunk_second_kernel,
            (PLANE * rows + down_weight.shape[0] * 3 // 4, 2 * LOCAL_FF),
            gateup_halves,
            down_halves,
        )
    else:
        mark = down_halves[0]

    dh_near = plane_near(grp, grad_residual.astype(BF16))
    dp_blocks, dn1_parts, stats = ([None] * PLANE for _ in range(3))
    for r in (0, 1, 2, 3):
        if r == 1:
            dh_blocks = plane_far(grp, dh_near)
        block = tie(dh_near[0], mark) if r == 0 else tie(dh_blocks[r], dp_blocks[r - 1])
        dp_blocks[r], dn1_parts[r], stats[r] = call(
            attend_back_kernel,
            (
                struct((length, 3 * LOCAL_Q), BF16),
                struct((length, width), BF16),
                struct((2, HEAD), F32),
            ),
            (
                block,
                projected[r],
                qkv_full,
                out_full,
                lam,
                hg,
            ),
            scratch=(pltpu.VMEM((length, LOCAL_Q), F32),),
            flops=2 * length * width * 5 * LOCAL_Q,
        )
    y_got = plane_scatter_first(grp, [tie(part, dp_blocks[1]) for part in y_parts], 1)
    qkv_halves = weight_grad(grp, normed_one, dp_blocks, PLANE)
    out_halves = weight_grad(grp, merged, dh_blocks, 1)
    y_terms, y_sent = plane_scatter_second(grp, y_parts, 1, tie(y_got, qkv_halves[0]))
    dn1_got = plane_scatter_first(grp, dn1_parts, 2)
    if tuned:
        mark, first_sum = spread(
            grp,
            chunk_first_kernel,
            (rows, PLANE * 3 * LOCAL_Q + width),
            [tie(qkv_halves[0], y_sent), *qkv_halves[1:]],
            out_halves,
        )
    else:
        mark = out_halves[0]
    late = lambda terms, mark: [terms[0]] + [tie(term, mark) for term in terms[1:]]

    if tuned:
        gateup_pieces, down_grad = owner(
            grp,
            owner_second_kernel,
            tie(second_sum, mark),
            (rows, 2 * LOCAL_FF),
            down_weight.shape,
        )
    else:
        down_grad, out_grad = owner_plain(grp, down_halves)[0], owner_plain(grp, out_halves)[0]
        gateup_pieces, qkv_pieces = (
            [
                lax.dynamic_index_in_dim(value, grp.j ^ r, 0, keepdims=False).astype(BF16)
                for r in range(PLANE)
            ]
            for value in (owner_plain(grp, gateup_halves), owner_plain(grp, qkv_halves))
        )
    dn1_terms, dn1_sent = plane_scatter_second(grp, dn1_parts, 2, tie(dn1_got, gateup_pieces[0]))
    stat = grp.everyone(add_up([tie(stats[0], gateup_pieces[0]), *stats[1:]]))
    layer_output = (residual + add_up(late(y_terms, dn1_sent))).astype(BF16)
    *gateup_res, gateup_dot = adam_columns(
        grp, late(exchange(grp, gateup_pieces), layer_output), gateup_weight, gateup_first, gateup_second, 2
    )
    input_grad = grad_residual + norm_back(
        add_up(late(dn1_terms, gateup_dot)), activations, gain_one
    )
    if tuned:
        qkv_pieces, out_grad = owner(
            grp,
            owner_first_kernel,
            tie(first_sum, input_grad, gateup_dot, stat),
            (rows, 3 * LOCAL_Q),
            out_weight.shape,
        )
    *qkv_res, qkv_dot = adam_columns(
        grp, exchange(grp, qkv_pieces), qkv_weight, qkv_first, qkv_second, 3
    )
    total_head, total_mixing = stat[0], stat[1, 0]
    gains_grad = jnp.concatenate([qkv_dot[:1], gateup_dot[:1]]) / gains_low.astype(F32)
    lambdas_grad = jnp.stack(
        [
            total_mixing * first_term * lambdas[1],
            total_mixing * first_term * lambdas[0],
            -total_mixing * second_term * lambdas[3],
            -total_mixing * second_term * lambdas[2],
        ]
    )
    out_res = adam_update(out_weight, out_first, out_second, out_grad, RATE_MATRIX, WEIGHT_DECAY)
    down_res = adam_update(
        down_weight, down_first, down_second, down_grad, RATE_MATRIX, WEIGHT_DECAY
    )
    gains_res = adam_update(norm_gains, gains_first, gains_second, gains_grad, RATE_GAIN, 0.0)
    lambdas_res = adam_update(
        lambdas, lambdas_first, lambdas_second, lambdas_grad, RATE_LAMBDA, 0.0
    )
    head_res = adam_update(head_gain, head_first, head_second, total_head, RATE_GAIN, 0.0)
    return (
        layer_output,
        input_grad,
        *qkv_res,
        *out_res,
        *gateup_res,
        *down_res,
        *gains_res,
        *lambdas_res,
        *head_res,
    )


def solution(mesh):
    members, d = mesh.shape["fsdp"] // PLANE, mesh.shape["dp"]
    inner = Mesh(mesh.devices.reshape(PLANE, members, d), AXES)
    rows, cols, whole = P(AXES, None), P(None, AXES), P()
    return jax.shard_map(
        functools.partial(per_device, members, d),
        mesh=inner,
        in_specs=(rows, rows, P(AXES)) + (rows,) * 12 + (cols,) * 3 + (whole,) * 6,
        out_specs=(rows,) * 14 + (cols,) * 3 + (whole,) * 6,
        check_vma=False,
    )
```

```python
import functools

import jax
import jax.numpy as jnp
from jax import lax
from jax.experimental import pallas as pl
from jax.experimental.pallas import tpu as pltpu
from jax.sharding import Mesh
from jax.sharding import PartitionSpec as P

HEADS = 12
HDIM = 64
HEAD = 2 * HDIM
FF = 4096
STEP = 10
PLANE = 4
LOCAL_HEADS = HEADS // PLANE
LOCAL_FF = FF // PLANE
LOCAL_Q = LOCAL_HEADS * HEAD

NORM_EPSILON = 1e-05
LAMBDA_INIT = 0.2
FACTOR = 1.0 - LAMBDA_INIT
BETA_FIRST = 0.9
BETA_SECOND = 0.95
ADAM_EPSILON = 1e-08
WEIGHT_DECAY = 0.1
RATE_MATRIX = 0.02
RATE_GAIN = 0.5
RATE_LAMBDA = 0.15
MASKED = -1000000000.0
SCALE = HDIM ** (-0.5)

BF16 = jnp.bfloat16
F32 = jnp.float32
VMEM_LIMIT = 28 * 1024 * 1024
AXES = ("j", "c", "dp")


def rms_scale(values):
    return lax.rsqrt(jnp.mean(values * values, axis=-1, keepdims=True) + NORM_EPSILON)


def mm(left, right):
    return lax.dot_general(left, right, (((1,), (0,)), ((), ())), preferred_element_type=F32)


def mm_nt(left, right):
    return lax.dot_general(left, right, (((1,), (1,)), ((), ())), preferred_element_type=F32)


def mm_tn(left, right):
    return lax.dot_general(left, right, (((0,), (0,)), ((), ())), preferred_element_type=F32)


def softmax_pair(q, k, rows):
    first = lax.broadcasted_iota(jnp.int32, (rows, HEAD), 1) < HDIM
    allowed = lax.broadcasted_iota(jnp.int32, (rows, rows), 0) >= lax.broadcasted_iota(
        jnp.int32, (rows, rows), 1
    )
    zero = jnp.zeros_like(q)
    result = []
    for half in (jnp.where(first, q, zero), jnp.where(first, zero, q)):
        scores = jnp.where(allowed, mm_nt(half, k) * SCALE, MASKED)
        terms = jnp.exp(scores - jnp.max(scores, axis=-1, keepdims=True))
        result.append(terms * (1.0 / jnp.sum(terms, axis=-1, keepdims=True)))
    return result


def attend_kernel(x_ref, gain_ref, wq_ref, wo_ref, lam_ref, hg_ref, n_ref, p_ref, g_ref, o_ref):
    rows = x_ref.shape[0]
    x = x_ref[...].astype(F32)
    n_ref[...] = (x * rms_scale(x) * gain_ref[...]).astype(BF16)
    for part in range(3):
        cols = pl.ds(part * LOCAL_Q, LOCAL_Q)
        p_ref[:, cols] = mm(n_ref[...], wq_ref[:, cols]).astype(BF16)
    lam = lam_ref[0, 0]
    for head in range(LOCAL_HEADS):
        q, k, v = (
            p_ref[:, pl.ds(part * LOCAL_Q + head * HEAD, HEAD)] for part in range(3)
        )
        a1, a2 = softmax_pair(q, k, rows)
        mixed = (a1 - lam * a2).astype(BF16)
        out = mm(mixed, v)
        g_ref[:, pl.ds(head * HEAD, HEAD)] = (
            out * rms_scale(out) * hg_ref[...] * FACTOR
        ).astype(BF16)
    o_ref[...] = mm(g_ref[...], wo_ref[...]).astype(BF16)


def join(refs):
    return jnp.concatenate([ref[...] for ref in refs], axis=0)


def part_of(refs, value):
    length = refs[0].shape[0]
    for i, ref in enumerate(refs):
        ref[...] = value[i * length : (i + 1) * length]


def down_blocks(rows):
    tall, block = rows * 3 // 4, 512
    cuts = sorted({*range(0, 3 * rows + 1, rows), *range(0, 3 * rows + 1, tall)})
    for at, stop in zip(cuts, cuts[1:]):
        yield at % rows, at // rows * block, at % tall, at // tall * block, stop - at


def pick(pos, pieces, k):
    m = len(pieces)
    value = pieces[0]
    for i in range(1, m):
        value = jnp.where((pos + k) % m == i, pieces[i], value)
    return value


def hidden_kernel(count, m, pos_ref, *refs):
    n_refs, (wgu_ref, h_ref, gate_ref, up_ref, *outs) = refs[:count], refs[count:]
    normed = join(n_refs)
    gate = mm(normed, wgu_ref[:, :LOCAL_FF])
    up = mm(normed, wgu_ref[:, LOCAL_FF:])
    sig = 0.5 * jnp.tanh(0.5 * gate) + 0.5
    silu = gate * sig
    h_ref[...] = (silu * up).astype(BF16)
    gate_ref[...] = (up * (sig + silu * (1.0 - sig))).astype(BF16)
    up_ref[...] = silu.astype(BF16)
    split_columns(m, pos_ref[1], normed, outs)


def split_columns(m, c, value, outs):
    width = value.shape[1] // PLANE
    share = width // m
    for k in range(m):
        columns = []
        for j in range(PLANE):
            pieces = [
                value[:, j * width + i * share : j * width + (i + 1) * share] for i in range(m)
            ]
            columns.append(pick(c, pieces, k))
        outs[k][...] = jnp.concatenate(columns, axis=1)


def hidden_back_kernel(count, *refs):
    dy_refs, (gate_ref, up_ref, wgu_ref, wd_ref, *outs, grad_ref) = refs[:count], refs[count:]
    dh = mm_nt(join(dy_refs), wd_ref[...])
    grad_ref[:, :LOCAL_FF] = (dh * gate_ref[...].astype(F32)).astype(BF16)
    grad_ref[:, LOCAL_FF:] = (dh * up_ref[...].astype(F32)).astype(BF16)
    part_of(outs, mm_nt(grad_ref[...], wgu_ref[...]).astype(BF16))


def down_grad_kernel(count, m, pos_ref, *refs):
    h_refs, dy_refs, outs = refs[:count], refs[count:-m], refs[-m:]
    per = len(dy_refs) // count
    share = outs[0].shape[0]
    for k in range(m):
        cols = pl.ds(pl.multiple_of((pos_ref[1] + k) % m * share, HEAD), share)
        value = sum(
            mm_tn(h_refs[i][:, cols], join(dy_refs[i * per : (i + 1) * per])) for i in range(count)
        )
        outs[k][...] = value.astype(BF16)


def second_grad_kernel(count, down_terms, *refs):
    lefts, rights, downs, out = (
        refs[:count],
        refs[count : 2 * count],
        refs[2 * count : 2 * count + down_terms],
        refs[-1],
    )
    d, tile = out.shape[0], 512
    tall = downs[0].shape[0] // d
    rows = lefts[0].shape[1] // PLANE // d
    for at in range(0, rights[0].shape[1], tile):
        cols = slice(at, at + tile)
        value = sum(mm_tn(left[...], right[:, cols]) for left, right in zip(lefts, rights))
        value = value.astype(BF16)
        for z in range(d):
            for j in range(PLANE):
                start = (j * d + z) * rows
                out[z, j * rows : (j + 1) * rows, cols] = value[start : start + rows]
    for z in range(d):
        value = add_up([term[z * tall : (z + 1) * tall, :] for term in downs]).astype(BF16)
        for row, col, to_row, to_col, size in down_blocks(tall):
            out[z, PLANE * rows + to_row : PLANE * rows + to_row + size, to_col : to_col + 512] = (
                value[row : row + size, col : col + 512]
            )


def down_kernel(count, *refs):
    h_refs, wd_ref, (own_ref, two_ref, message_ref) = refs[:count], refs[count], refs[count + 1 :]
    length = own_ref.shape[0]
    for i, (even_ref, h_ref) in enumerate(zip((own_ref, two_ref), h_refs)):
        value = mm(h_ref[...], wd_ref[...]).astype(BF16)
        even_ref[...] = value[:length]
        message_ref[i * length : (i + 1) * length, :] = value[length:]


def attend_back_kernel(
    dh_ref, p_ref, wq_ref, wo_ref, lam_ref, hg_ref, dp_ref, dn_ref, stat_ref, dg_ref
):
    rows = dh_ref.shape[0]
    dg_ref[...] = mm_nt(dh_ref[...], wo_ref[...])
    lam = lam_ref[0, 0]
    hg = hg_ref[...]
    first = lax.broadcasted_iota(jnp.int32, (rows, HEAD), 1) < HDIM
    grad_hg = jnp.zeros((1, HEAD), F32)
    grad_lam = jnp.zeros((1, 1), F32)
    for head in range(LOCAL_HEADS):
        q, k, v = (
            p_ref[:, pl.ds(part * LOCAL_Q + head * HEAD, HEAD)] for part in range(3)
        )
        a1, a2 = softmax_pair(q, k, rows)
        mixed = (a1 - lam * a2).astype(BF16)
        out = mm(mixed, v)
        scale = rms_scale(out)
        unit = out * scale
        dg = dg_ref[:, pl.ds(head * HEAD, HEAD)]
        grad_hg = grad_hg + FACTOR * jnp.sum(dg * unit, axis=0, keepdims=True)
        u = dg * hg * FACTOR
        dout = (scale * (u - unit * jnp.mean(u * unit, axis=-1, keepdims=True))).astype(BF16)
        dv = mm_tn(mixed, dout)
        dm = mm_nt(dout, v)
        dot1 = jnp.sum(dm * a1, axis=-1, keepdims=True)
        dot2 = jnp.sum(dm * a2, axis=-1, keepdims=True)
        grad_lam = grad_lam - jnp.sum(dot2, axis=0, keepdims=True)
        ds1 = (a1 * (dm - dot1)).astype(BF16)
        ds2 = (-lam * a2 * (dm - dot2)).astype(BF16)
        dq = jnp.where(first, mm(ds1, k), mm(ds2, k)) * SCALE
        dk = jnp.where(first, mm_tn(ds1, q), mm_tn(ds2, q)) * SCALE
        for part, value in enumerate((dq, dk, dv)):
            dp_ref[:, pl.ds(part * LOCAL_Q + head * HEAD, HEAD)] = value.astype(BF16)
    stat_ref[0:1, :] = grad_hg
    stat_ref[1:2, :] = jnp.broadcast_to(grad_lam, (1, HEAD))
    dn_ref[...] = mm_nt(dp_ref[...], wq_ref[:, : 3 * LOCAL_Q]).astype(BF16)


def split_kernel(parts, pos_ref, w_ref, *refs):
    gain_refs, outs = refs[:-PLANE], refs[-PLANE:]
    width = w_ref.shape[1] // parts
    quarter = width // PLANE
    rows = w_ref.shape[0]
    for r, out in enumerate(outs):
        q = pos_ref[0] ^ r
        for part in range(parts):
            cols = pl.ds(pl.multiple_of(part * width + q * quarter, HEAD), quarter)
            out[:, part * quarter : (part + 1) * quarter] = w_ref[:, cols].astype(BF16)
        for gain_ref in gain_refs:
            gains = jnp.concatenate([gain_ref[...], jnp.zeros((HEAD - 2, rows), F32)], axis=0).T
            out[:, parts * quarter :] = gains.astype(BF16)


def message_kernel(slot_ref, *refs):
    pieces, (weight_ref, out_ref, sem) = refs[:PLANE], refs[PLANE:]
    wide = pieces[0].shape[1]
    copies = []
    for r in range(PLANE):
        cols = pl.ds(pl.multiple_of(slot_ref[r] * wide, HEAD), wide)
        copies.append((pieces[r], out_ref.at[:, cols]))
    copy_all(copies, sem, lambda: store_low(out_ref, PLANE * wide, weight_ref))


def stack_kernel(slot_ref, *refs):
    pieces, (out_ref, sem) = refs[:PLANE], refs[PLANE:]
    copy_all([(pieces[r], out_ref.at[slot_ref[r]]) for r in range(PLANE)], sem)


def store_low(out_ref, start, in_ref):
    out_ref[:, start:] = in_ref[...].astype(BF16)


def copy_all(pairs, sem, meanwhile=lambda: None):
    copies = [pltpu.make_async_copy(a, b, sem.at[i]) for i, (a, b) in enumerate(pairs)]
    for copy in copies:
        copy.start()
    meanwhile()
    for copy in copies:
        copy.wait()


def place_second_kernel(in_ref, out_ref, sem):
    copy_all([(in_ref.at[k], out_ref.at[:, k]) for k in range(in_ref.shape[0])], sem)


def place_first_kernel(in_ref, qkv_ref, out_ref, gain_ref, sem):
    count, (rows, wide) = in_ref.shape[0], qkv_ref.shape[2:]
    copies = []
    for k in range(count):
        for j in range(PLANE):
            copies.append((in_ref.at[k, :, pl.ds(j * wide, wide)], qkv_ref.at[j, k]))
        copies.append((in_ref.at[k, :, pl.ds(PLANE * wide, out_ref.shape[2])], out_ref.at[k]))
    copy_all(copies, sem)
    columns = qkv_ref[:, :, :, 3 * LOCAL_Q :].astype(F32).reshape(PLANE * count * rows, HEAD)
    gain_ref[...] = columns.T[:8]


def weight_grad_kernel(m, pos_ref, *refs):
    lefts, rights, outs = refs[:PLANE], refs[PLANE : 2 * PLANE], refs[2 * PLANE : 2 * PLANE + m]
    left, right, total, sem = refs[2 * PLANE + m :]
    length = lefts[0].shape[0]
    copies = []
    for r in range(PLANE):
        for i, (src, dst) in enumerate(((lefts[r], left), (rights[r], right))):
            copies.append(
                pltpu.make_async_copy(
                    src, dst.at[pl.ds(r * length, length)], sem.at[2 * r + i]
                )
            )
            copies[-1].start()
    for copy in copies:
        copy.wait()
    rows, columns = total.shape
    share = rows // m
    for lead in range(outs[0].shape[0]):
        value = mm_tn(left[:, lead * rows : (lead + 1) * rows], right[...])
        if m == 2:
            top, low = value[:share].astype(BF16), value[share:].astype(BF16)
            outs[0][lead] = jnp.where(pos_ref[1] == 0, top, low)
            outs[1][lead] = jnp.where(pos_ref[1] == 0, low, top)
        else:
            total[...] = value
            for k in range(m):
                start = pl.multiple_of(((pos_ref[1] + k) % m) * share, 8)
                outs[k][lead] = total[pl.ds(start, share), :].astype(BF16)


def chunk_first_kernel(m, *refs):
    qkv, out_terms, out = refs[:m], refs[m : 2 * m], refs[2 * m]
    d, rows, _ = out.shape
    wide = qkv[0].shape[2]
    for z in range(d):
        for j in range(PLANE + 1):
            terms, lead = (qkv, j) if j < PLANE else (out_terms, 0)
            value = add_up([term[lead, z * rows : (z + 1) * rows, :] for term in terms])
            out[z, :, j * wide : j * wide + value.shape[1]] = value.astype(BF16)


def owner_first_kernel(pos_ref, in_ref, *outs):
    *outs, out_ref = outs
    wide = outs[0].shape[1]
    for r in range(PLANE):
        outs[r][...] = in_ref[:, pl.ds(pl.multiple_of((pos_ref[0] ^ r) * wide, HEAD), wide)]
    out_ref[...] = in_ref[:, PLANE * wide :].astype(F32)


def owner_second_kernel(pos_ref, in_ref, *outs):
    *outs, down_ref = outs
    rows, tall = outs[0].shape[0], down_ref.shape[0]
    for r in range(PLANE):
        q = pos_ref[0] ^ r
        if rows % 16 == 0:
            outs[r][...] = in_ref[pl.ds(pl.multiple_of(q * rows, 16), rows), :]
        else:
            outs[r][...] = pick(q, [in_ref[i * rows : (i + 1) * rows, :] for i in range(PLANE)], 0)
    for row, col, to_row, to_col, size in down_blocks(tall):
        down_ref[row : row + size, col : col + 512] = in_ref[
            PLANE * rows + to_row : PLANE * rows + to_row + size, to_col : to_col + 512
        ].astype(F32)


def adam_columns_kernel(parts, width, pos_ref, *refs):
    pieces, (w_ref, f_ref, s_ref, wn_ref, fn_ref, sn_ref, dot_ref) = refs[:PLANE], refs[PLANE:]
    quarter = width // PLANE
    dot = jnp.zeros((w_ref.shape[0], 1), F32)
    for r in range(PLANE):
        q = pos_ref[0] ^ r
        for part in range(parts):
            cols = pl.ds(pl.multiple_of(part * width + q * quarter, HEAD), quarter)
            grad = pieces[r][:, part * quarter : (part + 1) * quarter].astype(F32)
            weight = w_ref[:, cols]
            dot = dot + jnp.sum(weight.astype(BF16).astype(F32) * grad, axis=1, keepdims=True)
            wn_ref[:, cols], fn_ref[:, cols], sn_ref[:, cols] = adam_update(
                weight, f_ref[:, cols], s_ref[:, cols], grad, RATE_MATRIX, WEIGHT_DECAY
            )
    dot_ref[...] = jnp.broadcast_to(dot, (dot.shape[0], HEAD)).T[:8]


ANY = pl.BlockSpec(memory_space=pl.ANY)
VMEM = pl.BlockSpec(memory_space=pltpu.VMEM)
SMEM = pl.BlockSpec(memory_space=pltpu.SMEM)


COSTS = {
    split_kernel: 1.0,
    message_kernel: 1.5,
    stack_kernel: 1.0,
    place_first_kernel: 2.0,
    attend_kernel: 3.5,
    place_second_kernel: 3.0,
    hidden_kernel: 5.0,
    down_grad_kernel: 4.0,
    hidden_back_kernel: 5.0,
    second_grad_kernel: 7.5,
    down_kernel: 4.5,
    attend_back_kernel: 5.0,
    weight_grad_kernel: 5.0,
    chunk_first_kernel: 2.0,
    owner_first_kernel: 1.0,
    owner_second_kernel: 1.0,
    adam_columns_kernel: 4.0,
}


def call(kernel, outs, operands, scratch=(), flops=0, specs=None, out_spec=VMEM):
    size = sum(a.size * a.dtype.itemsize for a in operands) + sum(
        o.size * o.dtype.itemsize for o in outs
    )
    return pl.pallas_call(
        kernel,
        out_shape=tuple(outs),
        in_specs=specs or [VMEM] * len(operands),
        out_specs=(out_spec,) * len(outs),
        scratch_shapes=list(scratch),
        compiler_params=pltpu.CompilerParams(vmem_limit_bytes=VMEM_LIMIT),
        cost_estimate=pl.CostEstimate(flops=int(COSTS[getattr(kernel, "func", kernel)] * 1.15e9), bytes_accessed=0, transcendentals=0),
    )(*operands)


def shaped(*shape, dtype=BF16):
    return jax.ShapeDtypeStruct(shape, dtype)


def tie(value, *after):
    return lax.optimization_barrier((value, *after))[0]


class Group:
    def __init__(self, m, d):
        self.m, self.d = m, d
        self.j, self.c, self.z = (lax.axis_index(axis) for axis in AXES)
        self.pos = jnp.stack([self.j, self.c, self.z]).astype(jnp.int32)

    def plane(self, value, r):
        return lax.ppermute(value, "j", [(i, i ^ r) for i in range(PLANE)])

    def core(self, value, k):
        return lax.ppermute(value, "c", [(i, (i + k) % self.m) for i in range(self.m)])

    def everyone(self, value, step):
        n = PLANE * self.m * self.d
        return value + lax.ppermute(value, AXES, [(i, i ^ step) for i in range(n)])


def plane_near(grp, own):
    return [own, grp.plane(own, 1), grp.plane(own, 2)]


def plane_far(grp, near, *after):
    own, one, two = near
    half = own.shape[0] // 2
    top, low = grp.plane(one[:half], 2), grp.plane(two[half:], 1)
    if after:
        top, low = tie(top, *after), tie(low, *after)
    return [own, one, two, jnp.concatenate([top, low], axis=0)]


def plane_gather(grp, own):
    return plane_far(grp, plane_near(grp, own))


def plane_send(grp, parts):
    return [parts[0]] + [grp.plane(parts[r], r) for r in range(1, PLANE)]


def plane_scatter_second(grp, part, axis, got):
    sent = add_up([part, got[part.shape[0] :]]).astype(BF16)
    return sent, grp.plane(sent, 3 - axis)


def add_up(terms):
    return sum(term.astype(F32) for term in terms)


def exchange(grp, pieces):
    return [pieces[0]] + [grp.plane(pieces[r], r) for r in range(1, PLANE)]


def core_terms(grp, halves):
    return [halves[0]] + [grp.core(halves[k], k) for k in range(1, grp.m)]


def owner(grp, kernel, message, piece, rest=()):
    return call(
        kernel,
        (shaped(*piece),) * PLANE + rest,
        (grp.pos, message),
        specs=[SMEM, VMEM],
    )


def weight_grad(grp, lefts, rights, lead):
    length, rows = lefts[0].shape
    columns = rights[0].shape[1]
    share = rows // lead // grp.m
    return call(
        functools.partial(weight_grad_kernel, grp.m),
        (shaped(lead, share, columns),) * grp.m,
        (grp.pos, *lefts, *rights),
        scratch=(
            pltpu.VMEM((PLANE * length, rows), BF16),
            pltpu.VMEM((PLANE * length, columns), BF16),
            pltpu.VMEM((rows // lead, columns), F32),
            pltpu.SemaphoreType.DMA((2 * PLANE,)),
        ),
        specs=[SMEM] + [ANY] * (2 * PLANE),
        flops=2 * PLANE * length * rows * columns,
    )


def adam_columns(grp, pieces, weight, first, second, parts):
    rows, columns = weight.shape
    return call(
        functools.partial(adam_columns_kernel, parts, columns // parts),
        (shaped(rows, columns, dtype=F32),) * 3 + (shaped(8, rows, dtype=F32),),
        (grp.pos, *pieces, weight, first, second),
        specs=[SMEM] + [VMEM] * (PLANE + 3),
    )


def norm_back(grad_normed, values, gain):
    scale_rows = rms_scale(values)
    scaled = grad_normed * gain
    unit_rows = values * scale_rows
    return scale_rows * (
        scaled - unit_rows * jnp.mean(scaled * unit_rows, axis=-1, keepdims=True)
    )


def adam_update(weight, first, second, grad, rate, decay):
    first_new = BETA_FIRST * first + (1.0 - BETA_FIRST) * grad
    second_new = BETA_SECOND * second + (1.0 - BETA_SECOND) * grad * grad
    corrected_first = first_new / (1.0 - BETA_FIRST**STEP)
    corrected_second = second_new / (1.0 - BETA_SECOND**STEP)
    weight_new = weight - rate * (
        corrected_first / (jnp.sqrt(corrected_second) + ADAM_EPSILON) + decay * weight
    )
    return (weight_new, first_new, second_new)


def per_device(
    members,
    d,
    inputs,
    cotangent,
    needle,
    qkv_weight,
    qkv_first,
    qkv_second,
    out_weight,
    out_first,
    out_second,
    gateup_weight,
    gateup_first,
    gateup_second,
    down_weight,
    down_first,
    down_second,
    norm_gains,
    gains_first,
    gains_second,
    lambdas,
    lambdas_first,
    lambdas_second,
    head_gain,
    head_first,
    head_second,
):
    grp = Group(members, d)
    length, width = inputs.shape
    rows = qkv_weight.shape[0]

    gains_low = norm_gains.astype(BF16)
    plane_slots = jnp.stack([grp.j ^ r for r in range(PLANE)]).astype(jnp.int32)
    wide = 3 * LOCAL_Q + HEAD
    count = members * d
    everywhere = functools.partial(lax.all_gather, axis_name=("c", "dp"), axis=0, tiled=False)
    to_owner = functools.partial(lax.psum_scatter, axis_name="dp", scatter_dimension=0, tiled=False)
    late = lambda terms, *marks: [terms[0]] + [tie(term, *marks) for term in terms[1:]]
    first_quarters = call(
        functools.partial(split_kernel, 3),
        (shaped(rows, wide),) * PLANE,
        (grp.pos, qkv_weight, norm_gains),
        specs=[SMEM] + [VMEM] * 2,
    )
    first_message = call(
        message_kernel,
        (shaped(rows, PLANE * wide + width),),
        (plane_slots, *exchange(grp, first_quarters), out_weight),
        scratch=(pltpu.SemaphoreType.DMA((PLANE,)),),
        specs=[SMEM] + [ANY] * PLANE + [VMEM],
    )[0]
    second_quarters = call(
        functools.partial(split_kernel, 2),
        (shaped(rows, 2 * LOCAL_FF),) * PLANE,
        (grp.pos, tie(gateup_weight, first_quarters[0])),
        specs=[SMEM, VMEM],
    )
    second_message = call(
        stack_kernel,
        (shaped(PLANE, rows, 2 * LOCAL_FF),),
        (plane_slots, *exchange(grp, second_quarters)),
        scratch=(pltpu.SemaphoreType.DMA((PLANE,)),),
        specs=[SMEM] + [ANY] * PLANE,
    )[0]
    first_all = everywhere(first_message)
    x_near = plane_near(grp, tie(inputs, first_message))
    second_all = everywhere(tie(second_message, *x_near[1:]))
    x_blocks = plane_far(grp, x_near)
    down_all = everywhere(tie(down_weight, x_blocks[3]).astype(BF16))
    grad_out = cotangent.astype(F32) * needle.astype(F32)[:, None]
    dy_blocks = plane_gather(grp, tie(grad_out, x_blocks[3]).astype(BF16))
    qkv_full, out_full, gains_full = call(
        place_first_kernel,
        (
            shaped(PLANE, count, rows, wide),
            shaped(count, rows, width),
            shaped(8, width, dtype=F32),
        ),
        (tie(first_all, *dy_blocks[1:]),),
        scratch=(pltpu.SemaphoreType.DMA((count * (PLANE + 1),)),),
        specs=[ANY],
    )
    qkv_full, out_full = qkv_full.reshape(width, wide), out_full.reshape(LOCAL_Q, width)
    gain_one, gain_two = gains_full[0:1], gains_full[1:2]
    first_term = jnp.exp(jnp.sum(lambdas[0] * lambdas[1]))
    second_term = jnp.exp(jnp.sum(lambdas[2] * lambdas[3]))
    mixing = first_term - second_term + LAMBDA_INIT
    lam = jnp.broadcast_to(mixing, (1, HEAD))
    hg = head_gain.reshape(1, HEAD)

    activations = inputs.astype(F32)
    normed_one, projected, merged, parts = ([None] * PLANE for _ in range(4))
    for r in (3, 1, 2, 0):
        normed_one[r], projected[r], merged[r], parts[r] = call(
            attend_kernel,
            (
                shaped(length, width),
                shaped(length, 3 * LOCAL_Q),
                shaped(length, LOCAL_Q),
                shaped(length, width),
            ),
            (x_blocks[r], gain_one, qkv_full, out_full, lam, hg),
        )
    residual = activations + add_up(plane_send(grp, parts))
    normed_two = (residual * rms_scale(residual) * gain_two).astype(BF16)

    n2_near = plane_near(grp, normed_two)
    gateup_full = call(
        place_second_kernel,
        (shaped(PLANE, count, rows, 2 * LOCAL_FF),),
        (tie(second_all, normed_two),),
        scratch=(pltpu.SemaphoreType.DMA((count,)),),
        specs=[ANY],
    )[0].reshape(width, -1)
    n2_near[1:] = [tie(block, gateup_full) for block in n2_near[1:]]
    pairs = ((0, 1), (2, 3))
    flat = lambda lists: [item for items in lists for item in items]
    hidden, gate_factor, up_factor, lefts = ([] for _ in range(4))
    n2_blocks = n2_near
    for pair in pairs:
        if pair[1] == 3:
            n2_blocks = plane_far(grp, n2_near, hidden[0])
        h, gate, up, *columns = call(
            functools.partial(hidden_kernel, 2, members),
            (shaped(2 * length, LOCAL_FF),) * 3
            + (shaped(2 * length, width // members),) * members,
            (grp.pos, *(n2_blocks[r] for r in pair), gateup_full),
            specs=[SMEM] + [VMEM] * 3,
        )
        hidden.append(h)
        gate_factor.append(gate)
        up_factor.append(up)
        lefts.append(core_terms(grp, columns))

    down_halves = call(
        functools.partial(down_grad_kernel, 2, members),
        (shaped(LOCAL_FF // members, width),) * members,
        (grp.pos, *hidden, *dy_blocks),
        specs=[SMEM] + [VMEM] * (2 + PLANE),
    )
    down_full = tie(down_all, down_halves[0]).reshape(LOCAL_FF, width)
    dn2_terms, rights = [None] * PLANE, [None] * 2
    for i in (1, 0):
        pair = pairs[i]
        *sent, grad = call(
            functools.partial(hidden_back_kernel, 2),
            (shaped(length, width),) * 2 + (shaped(2 * length, 2 * LOCAL_FF),),
            (
                *(dy_blocks[r] for r in pair),
                tie(gate_factor[i], *flat(lefts)) if i else gate_factor[i],
                up_factor[i],
                gateup_full,
                down_full,
            ),
        )
        rights[i] = [grad] + [grp.core(grad, k) for k in range(1, members)]
        for r, block in zip(pair, sent):
            dn2_terms[r] = grp.plane(block, r) if r else block
    down_terms = core_terms(grp, down_halves)
    second_message = call(
        functools.partial(second_grad_kernel, 2 * members, members),
        (shaped(d, PLANE * rows + down_weight.shape[0] * 3 // 4, 2 * LOCAL_FF),),
        (*flat(lefts), *flat(rights), *down_terms),
    )[0]
    second_sum = to_owner(second_message)
    grad_residual = grad_out + norm_back(add_up(dn2_terms), residual, gain_two)

    dh_near = plane_near(grp, grad_residual.astype(BF16))
    dh_blocks = plane_far(grp, dh_near)
    y_parts = call(
        functools.partial(down_kernel, 2),
        (shaped(length, width),) * 2 + (shaped(2 * length, width),),
        (*hidden, tie(down_full, grad_residual)),
    )
    dp_blocks, dn1_parts, stats = ([None] * PLANE for _ in range(3))
    for r in range(PLANE):
        block = tie(dh_blocks[r], dp_blocks[r - 1] if r else y_parts[0])
        dp_blocks[r], dn1_parts[r], stats[r] = call(
            attend_back_kernel,
            (
                shaped(length, 3 * LOCAL_Q),
                shaped(length, width),
                shaped(2, HEAD, dtype=F32),
            ),
            (block, projected[r], qkv_full, out_full, lam, hg),
            scratch=(pltpu.VMEM((length, LOCAL_Q), F32),),
        )
    y_got = grp.plane(tie(y_parts[2], dp_blocks[0]), 1)
    qkv_halves = weight_grad(grp, normed_one, dp_blocks, PLANE)
    out_halves = weight_grad(grp, merged, dh_blocks, 1)
    half = PLANE * count // 2
    stat = grp.everyone(add_up(stats), half)
    dn1_got = grp.plane(tie(jnp.concatenate([dn1_parts[2], dn1_parts[3]], axis=0), stat), 2)
    step = half // 4
    while step:
        stat = grp.everyone(stat, step)
        step //= 2
    first_chunks = call(
        functools.partial(chunk_first_kernel, members),
        (shaped(d, rows, PLANE * 3 * LOCAL_Q + width),),
        (*core_terms(grp, qkv_halves), *core_terms(grp, out_halves)),
    )[0]
    first_sum = to_owner(first_chunks)

    *gateup_pieces, down_grad = owner(
        grp,
        owner_second_kernel,
        tie(second_sum, first_chunks),
        (rows, 2 * LOCAL_FF),
        (shaped(*down_weight.shape, dtype=F32),),
    )
    gateup_pieces = exchange(grp, gateup_pieces)
    y_got = tie(y_got, gateup_pieces[0])
    y_sent, y_last = plane_scatter_second(grp, y_parts[1], 1, y_got)
    dn1_got = tie(dn1_got, y_sent)
    dn1_sent, dn1_last = plane_scatter_second(grp, dn1_parts[1], 2, dn1_got)
    *gateup_res, gateup_dot = adam_columns(
        grp, late(gateup_pieces, dn1_sent), gateup_weight, gateup_first, gateup_second, 2
    )
    y_got, y_last = tie(y_got, gateup_dot), tie(y_last, gateup_dot)
    layer_output = (residual + add_up([y_parts[0], y_got[:length], y_last])).astype(BF16)
    stat = grp.everyone(tie(stat, dn1_sent), half // 2)
    dn1_got, dn1_last = tie(dn1_got, layer_output), tie(dn1_last, layer_output)
    input_grad = grad_residual + norm_back(
        add_up([dn1_parts[0], dn1_got[:length], dn1_last]), activations, gain_one
    )
    *qkv_pieces, out_grad = owner(
        grp,
        owner_first_kernel,
        tie(first_sum, input_grad, stat),
        (rows, 3 * LOCAL_Q),
        (shaped(*out_weight.shape, dtype=F32),),
    )
    *qkv_res, qkv_dot = adam_columns(
        grp, exchange(grp, qkv_pieces), qkv_weight, qkv_first, qkv_second, 3
    )
    total_head, total_mixing = stat[0], stat[1, 0]
    gains_grad = jnp.concatenate([qkv_dot[:1], gateup_dot[:1]]) / gains_low.astype(F32)
    lambdas_grad = jnp.stack(
        [
            total_mixing * first_term * lambdas[1],
            total_mixing * first_term * lambdas[0],
            -total_mixing * second_term * lambdas[3],
            -total_mixing * second_term * lambdas[2],
        ]
    )
    out_res = adam_update(out_weight, out_first, out_second, out_grad, RATE_MATRIX, WEIGHT_DECAY)
    down_res = adam_update(
        down_weight, down_first, down_second, down_grad, RATE_MATRIX, WEIGHT_DECAY
    )
    gains_res = adam_update(norm_gains, gains_first, gains_second, gains_grad, RATE_GAIN, 0.0)
    lambdas_res = adam_update(
        lambdas, lambdas_first, lambdas_second, lambdas_grad, RATE_LAMBDA, 0.0
    )
    head_res = adam_update(head_gain, head_first, head_second, total_head, RATE_GAIN, 0.0)
    return (
        layer_output,
        input_grad,
        *qkv_res,
        *out_res,
        *gateup_res,
        *down_res,
        *gains_res,
        *lambdas_res,
        *head_res,
    )


def solution(mesh):
    members, d = mesh.shape["fsdp"] // PLANE, mesh.shape["dp"]
    inner = Mesh(mesh.devices.reshape(PLANE, members, d), AXES)
    rows, cols, whole = P(AXES, None), P(None, AXES), P()
    return jax.shard_map(
        functools.partial(per_device, members, d),
        mesh=inner,
        in_specs=(rows, rows, P(AXES)) + (rows,) * 12 + (cols,) * 3 + (whole,) * 6,
        out_specs=(rows,) * 14 + (cols,) * 3 + (whole,) * 6,
        check_vma=False,
    )
```

```python
import functools

import jax
import jax.numpy as jnp
from jax import lax
from jax.experimental import pallas as pl
from jax.experimental.pallas import tpu as pltpu
from jax.sharding import Mesh
from jax.sharding import PartitionSpec as P

HEADS = 12
HDIM = 64
HEAD = 2 * HDIM
FF = 4096
STEP = 10
PLANE = 4
LOCAL_HEADS = HEADS // PLANE
LOCAL_FF = FF // PLANE
LOCAL_Q = LOCAL_HEADS * HEAD

NORM_EPSILON = 1e-05
LAMBDA_INIT = 0.2
FACTOR = 1.0 - LAMBDA_INIT
BETA_FIRST = 0.9
BETA_SECOND = 0.95
ADAM_EPSILON = 1e-08
WEIGHT_DECAY = 0.1
RATE_MATRIX = 0.02
RATE_GAIN = 0.5
RATE_LAMBDA = 0.15
MASKED = -1000000000.0
SCALE = HDIM ** (-0.5)

BF16 = jnp.bfloat16
F32 = jnp.float32
VMEM_LIMIT = 28 * 1024 * 1024
AXES = ("j", "c", "dp")


def rms_scale(values):
    return lax.rsqrt(jnp.mean(values * values, axis=-1, keepdims=True) + NORM_EPSILON)


def mm(left, right):
    return lax.dot_general(left, right, (((1,), (0,)), ((), ())), preferred_element_type=F32)


def mm_nt(left, right):
    return lax.dot_general(left, right, (((1,), (1,)), ((), ())), preferred_element_type=F32)


def mm_tn(left, right):
    return lax.dot_general(left, right, (((0,), (0,)), ((), ())), preferred_element_type=F32)


def softmax_pair(q, k, rows):
    first = lax.broadcasted_iota(jnp.int32, (rows, HEAD), 1) < HDIM
    allowed = lax.broadcasted_iota(jnp.int32, (rows, rows), 0) >= lax.broadcasted_iota(
        jnp.int32, (rows, rows), 1
    )
    zero = jnp.zeros_like(q)
    result = []
    for half in (jnp.where(first, q, zero), jnp.where(first, zero, q)):
        scores = jnp.where(allowed, mm_nt(half, k) * SCALE, MASKED)
        terms = jnp.exp(scores - jnp.max(scores, axis=-1, keepdims=True))
        result.append(terms * (1.0 / jnp.sum(terms, axis=-1, keepdims=True)))
    return result


def attend_kernel(x_ref, gain_ref, wq_ref, wo_ref, lam_ref, hg_ref, n_ref, p_ref, g_ref, o_ref):
    rows = x_ref.shape[0]
    x = x_ref[...].astype(F32)
    n_ref[...] = (x * rms_scale(x) * gain_ref[...]).astype(BF16)
    for part in range(3):
        cols = pl.ds(part * LOCAL_Q, LOCAL_Q)
        p_ref[:, cols] = mm(n_ref[...], wq_ref[:, cols]).astype(BF16)
    lam = lam_ref[0, 0]
    for head in range(LOCAL_HEADS):
        q, k, v = (
            p_ref[:, pl.ds(part * LOCAL_Q + head * HEAD, HEAD)] for part in range(3)
        )
        a1, a2 = softmax_pair(q, k, rows)
        mixed = (a1 - lam * a2).astype(BF16)
        out = mm(mixed, v)
        g_ref[:, pl.ds(head * HEAD, HEAD)] = (
            out * rms_scale(out) * hg_ref[...] * FACTOR
        ).astype(BF16)
    o_ref[...] = mm(g_ref[...], wo_ref[...]).astype(BF16)


def join(refs):
    return jnp.concatenate([ref[...] for ref in refs], axis=0)


def part_of(refs, value):
    length = refs[0].shape[0]
    for i, ref in enumerate(refs):
        ref[...] = value[i * length : (i + 1) * length]


def down_blocks(rows):
    tall, block = rows * 3 // 4, 512
    cuts = sorted({*range(0, 3 * rows + 1, rows), *range(0, 3 * rows + 1, tall)})
    for at, stop in zip(cuts, cuts[1:]):
        yield at % rows, at // rows * block, at % tall, at // tall * block, stop - at


def pick(pos, pieces, k):
    m = len(pieces)
    value = pieces[0]
    for i in range(1, m):
        value = jnp.where((pos + k) % m == i, pieces[i], value)
    return value


def hidden_kernel(count, m, pos_ref, *refs):
    n_refs, (wgu_ref, h_ref, gate_ref, up_ref, *outs) = refs[:count], refs[count:]
    normed = join(n_refs)
    gate = mm(normed, wgu_ref[:, :LOCAL_FF])
    up = mm(normed, wgu_ref[:, LOCAL_FF:])
    sig = 0.5 * jnp.tanh(0.5 * gate) + 0.5
    silu = gate * sig
    h_ref[...] = (silu * up).astype(BF16)
    gate_ref[...] = (up * (sig + silu * (1.0 - sig))).astype(BF16)
    up_ref[...] = silu.astype(BF16)
    split_columns(m, pos_ref[1], normed, outs)


def split_columns(m, c, value, outs):
    width = value.shape[1] // PLANE
    share = width // m
    for k in range(m):
        columns = []
        for j in range(PLANE):
            pieces = [
                value[:, j * width + i * share : j * width + (i + 1) * share] for i in range(m)
            ]
            columns.append(pick(c, pieces, k))
        outs[k][...] = jnp.concatenate(columns, axis=1)


def hidden_back_kernel(count, *refs):
    dy_refs, (gate_ref, up_ref, wgu_ref, wd_ref, *outs, grad_ref) = refs[:count], refs[count:]
    dh = mm_nt(join(dy_refs), wd_ref[...])
    grad_ref[:, :LOCAL_FF] = (dh * gate_ref[...].astype(F32)).astype(BF16)
    grad_ref[:, LOCAL_FF:] = (dh * up_ref[...].astype(F32)).astype(BF16)
    part_of(outs, mm_nt(grad_ref[...], wgu_ref[...]).astype(BF16))


def down_grad_kernel(count, m, pos_ref, *refs):
    h_refs, dy_refs, outs = refs[:count], refs[count:-m], refs[-m:]
    per = len(dy_refs) // count
    share = outs[0].shape[0]
    for k in range(m):
        cols = pl.ds(pl.multiple_of((pos_ref[1] + k) % m * share, HEAD), share)
        value = sum(
            mm_tn(h_refs[i][:, cols], join(dy_refs[i * per : (i + 1) * per])) for i in range(count)
        )
        outs[k][...] = value.astype(BF16)


def second_grad_kernel(count, down_terms, *refs):
    lefts, rights, downs, out = (
        refs[:count],
        refs[count : 2 * count],
        refs[2 * count : 2 * count + down_terms],
        refs[-1],
    )
    d, tile = out.shape[0], 512
    tall = downs[0].shape[0] // d
    rows = lefts[0].shape[1] // PLANE // d
    for at in range(0, rights[0].shape[1], tile):
        cols = slice(at, at + tile)
        value = sum(mm_tn(left[...], right[:, cols]) for left, right in zip(lefts, rights))
        value = value.astype(BF16)
        for z in range(d):
            for j in range(PLANE):
                start = (j * d + z) * rows
                out[z, j * rows : (j + 1) * rows, cols] = value[start : start + rows]
    for z in range(d):
        value = add_up([term[z * tall : (z + 1) * tall, :] for term in downs]).astype(BF16)
        for row, col, to_row, to_col, size in down_blocks(tall):
            out[z, PLANE * rows + to_row : PLANE * rows + to_row + size, to_col : to_col + 512] = (
                value[row : row + size, col : col + 512]
            )


def down_kernel(count, *refs):
    h_refs, wd_ref, (own_ref, two_ref, message_ref) = refs[:count], refs[count], refs[count + 1 :]
    length = own_ref.shape[0]
    for i, (even_ref, h_ref) in enumerate(zip((own_ref, two_ref), h_refs)):
        value = mm(h_ref[...], wd_ref[...]).astype(BF16)
        even_ref[...] = value[:length]
        message_ref[i * length : (i + 1) * length, :] = value[length:]


def attend_back_kernel(
    dh_ref, p_ref, wq_ref, wo_ref, lam_ref, hg_ref, dp_ref, dn_ref, stat_ref, dg_ref
):
    rows = dh_ref.shape[0]
    dg_ref[...] = mm_nt(dh_ref[...], wo_ref[...])
    lam = lam_ref[0, 0]
    hg = hg_ref[...]
    first = lax.broadcasted_iota(jnp.int32, (rows, HEAD), 1) < HDIM
    grad_hg = jnp.zeros((1, HEAD), F32)
    grad_lam = jnp.zeros((1, 1), F32)
    for head in range(LOCAL_HEADS):
        q, k, v = (
            p_ref[:, pl.ds(part * LOCAL_Q + head * HEAD, HEAD)] for part in range(3)
        )
        a1, a2 = softmax_pair(q, k, rows)
        mixed = (a1 - lam * a2).astype(BF16)
        out = mm(mixed, v)
        scale = rms_scale(out)
        unit = out * scale
        dg = dg_ref[:, pl.ds(head * HEAD, HEAD)]
        grad_hg = grad_hg + FACTOR * jnp.sum(dg * unit, axis=0, keepdims=True)
        u = dg * hg * FACTOR
        dout = (scale * (u - unit * jnp.mean(u * unit, axis=-1, keepdims=True))).astype(BF16)
        dv = mm_tn(mixed, dout)
        dm = mm_nt(dout, v)
        dot1 = jnp.sum(dm * a1, axis=-1, keepdims=True)
        dot2 = jnp.sum(dm * a2, axis=-1, keepdims=True)
        grad_lam = grad_lam - jnp.sum(dot2, axis=0, keepdims=True)
        ds1 = (a1 * (dm - dot1)).astype(BF16)
        ds2 = (-lam * a2 * (dm - dot2)).astype(BF16)
        dq = jnp.where(first, mm(ds1, k), mm(ds2, k)) * SCALE
        dk = jnp.where(first, mm_tn(ds1, q), mm_tn(ds2, q)) * SCALE
        for part, value in enumerate((dq, dk, dv)):
            dp_ref[:, pl.ds(part * LOCAL_Q + head * HEAD, HEAD)] = value.astype(BF16)
    stat_ref[0:1, :] = grad_hg
    stat_ref[1:2, :] = jnp.broadcast_to(grad_lam, (1, HEAD))
    dn_ref[...] = mm_nt(dp_ref[...], wq_ref[:, : 3 * LOCAL_Q]).astype(BF16)


def split_kernel(parts, pos_ref, w_ref, *refs):
    gain_refs, outs = refs[:-PLANE], refs[-PLANE:]
    width = w_ref.shape[1] // parts
    quarter = width // PLANE
    rows = w_ref.shape[0]
    for r, out in enumerate(outs):
        q = pos_ref[0] ^ r
        for part in range(parts):
            cols = pl.ds(pl.multiple_of(part * width + q * quarter, HEAD), quarter)
            out[:, part * quarter : (part + 1) * quarter] = w_ref[:, cols].astype(BF16)
        for gain_ref in gain_refs:
            gains = jnp.concatenate([gain_ref[...], jnp.zeros((HEAD - 2, rows), F32)], axis=0).T
            out[:, parts * quarter :] = gains.astype(BF16)


def message_kernel(slot_ref, *refs):
    pieces, (weight_ref, out_ref, sem) = refs[:PLANE], refs[PLANE:]
    wide = pieces[0].shape[1]
    copies = []
    for r in range(PLANE):
        cols = pl.ds(pl.multiple_of(slot_ref[r] * wide, HEAD), wide)
        copies.append((pieces[r], out_ref.at[:, cols]))
    copy_all(copies, sem, lambda: store_low(out_ref, PLANE * wide, weight_ref))


def stack_kernel(slot_ref, *refs):
    pieces, (out_ref, sem) = refs[:PLANE], refs[PLANE:]
    copy_all([(pieces[r], out_ref.at[slot_ref[r]]) for r in range(PLANE)], sem)


def store_low(out_ref, start, in_ref):
    out_ref[:, start:] = in_ref[...].astype(BF16)


def copy_all(pairs, sem, meanwhile=lambda: None):
    copies = [pltpu.make_async_copy(a, b, sem.at[i]) for i, (a, b) in enumerate(pairs)]
    for copy in copies:
        copy.start()
    meanwhile()
    for copy in copies:
        copy.wait()


def place_second_kernel(in_ref, out_ref, sem):
    copy_all([(in_ref.at[k], out_ref.at[:, k]) for k in range(in_ref.shape[0])], sem)


def place_first_kernel(in_ref, qkv_ref, out_ref, gain_ref, sem):
    count, (rows, wide) = in_ref.shape[0], qkv_ref.shape[2:]
    copies = []
    for k in range(count):
        for j in range(PLANE):
            copies.append((in_ref.at[k, :, pl.ds(j * wide, wide)], qkv_ref.at[j, k]))
        copies.append((in_ref.at[k, :, pl.ds(PLANE * wide, out_ref.shape[2])], out_ref.at[k]))
    copy_all(copies, sem)
    columns = qkv_ref[:, :, :, 3 * LOCAL_Q :].astype(F32).reshape(PLANE * count * rows, HEAD)
    gain_ref[...] = columns.T[:8]


def weight_grad_kernel(m, pos_ref, *refs):
    lefts, rights, outs = refs[:PLANE], refs[PLANE : 2 * PLANE], refs[2 * PLANE : 2 * PLANE + m]
    left, right, total, sem = refs[2 * PLANE + m :]
    length = lefts[0].shape[0]
    copies = []
    for r in range(PLANE):
        for i, (src, dst) in enumerate(((lefts[r], left), (rights[r], right))):
            copies.append(
                pltpu.make_async_copy(
                    src, dst.at[pl.ds(r * length, length)], sem.at[2 * r + i]
                )
            )
            copies[-1].start()
    for copy in copies:
        copy.wait()
    rows, columns = total.shape
    share = rows // m
    for lead in range(outs[0].shape[0]):
        value = mm_tn(left[:, lead * rows : (lead + 1) * rows], right[...])
        if m == 2:
            top, low = value[:share].astype(BF16), value[share:].astype(BF16)
            outs[0][lead] = jnp.where(pos_ref[1] == 0, top, low)
            outs[1][lead] = jnp.where(pos_ref[1] == 0, low, top)
        else:
            total[...] = value
            for k in range(m):
                start = pl.multiple_of(((pos_ref[1] + k) % m) * share, 8)
                outs[k][lead] = total[pl.ds(start, share), :].astype(BF16)


def chunk_first_kernel(m, *refs):
    qkv, out_terms, out = refs[:m], refs[m : 2 * m], refs[2 * m]
    d, rows, _ = out.shape
    wide = qkv[0].shape[2]
    for z in range(d):
        for j in range(PLANE + 1):
            terms, lead = (qkv, j) if j < PLANE else (out_terms, 0)
            value = add_up([term[lead, z * rows : (z + 1) * rows, :] for term in terms])
            out[z, :, j * wide : j * wide + value.shape[1]] = value.astype(BF16)


def owner_first_kernel(pos_ref, in_ref, *outs):
    *outs, out_ref = outs
    wide = outs[0].shape[1]
    for r in range(PLANE):
        outs[r][...] = in_ref[:, pl.ds(pl.multiple_of((pos_ref[0] ^ r) * wide, HEAD), wide)]
    out_ref[...] = in_ref[:, PLANE * wide :].astype(F32)


def owner_second_kernel(pos_ref, in_ref, *outs):
    *outs, down_ref = outs
    rows, tall = outs[0].shape[0], down_ref.shape[0]
    for r in range(PLANE):
        q = pos_ref[0] ^ r
        if rows % 16 == 0:
            outs[r][...] = in_ref[pl.ds(pl.multiple_of(q * rows, 16), rows), :]
        else:
            outs[r][...] = pick(q, [in_ref[i * rows : (i + 1) * rows, :] for i in range(PLANE)], 0)
    for row, col, to_row, to_col, size in down_blocks(tall):
        down_ref[row : row + size, col : col + 512] = in_ref[
            PLANE * rows + to_row : PLANE * rows + to_row + size, to_col : to_col + 512
        ].astype(F32)


def adam_columns_kernel(parts, width, pos_ref, *refs):
    pieces, (w_ref, f_ref, s_ref, wn_ref, fn_ref, sn_ref, dot_ref) = refs[:PLANE], refs[PLANE:]
    quarter = width // PLANE
    dot = jnp.zeros((w_ref.shape[0], 1), F32)
    for r in range(PLANE):
        q = pos_ref[0] ^ r
        for part in range(parts):
            cols = pl.ds(pl.multiple_of(part * width + q * quarter, HEAD), quarter)
            grad = pieces[r][:, part * quarter : (part + 1) * quarter].astype(F32)
            weight = w_ref[:, cols]
            dot = dot + jnp.sum(weight.astype(BF16).astype(F32) * grad, axis=1, keepdims=True)
            wn_ref[:, cols], fn_ref[:, cols], sn_ref[:, cols] = adam_update(
                weight, f_ref[:, cols], s_ref[:, cols], grad, RATE_MATRIX, WEIGHT_DECAY
            )
    dot_ref[...] = jnp.broadcast_to(dot, (dot.shape[0], HEAD)).T[:8]


ANY = pl.BlockSpec(memory_space=pl.ANY)
VMEM = pl.BlockSpec(memory_space=pltpu.VMEM)
SMEM = pl.BlockSpec(memory_space=pltpu.SMEM)


COSTS = {
    split_kernel: 1.0,
    message_kernel: 1.5,
    stack_kernel: 1.0,
    place_first_kernel: 2.0,
    attend_kernel: 3.5,
    place_second_kernel: 3.0,
    hidden_kernel: 5.0,
    down_grad_kernel: 4.0,
    hidden_back_kernel: 5.0,
    second_grad_kernel: 7.5,
    down_kernel: 4.5,
    attend_back_kernel: 15,
    weight_grad_kernel: 5.0,
    chunk_first_kernel: 2.0,
    owner_first_kernel: 1.0,
    owner_second_kernel: 1.0,
    adam_columns_kernel: 4.0,
}


def call(kernel, outs, operands, scratch=(), flops=0, specs=None, out_spec=VMEM):
    size = sum(a.size * a.dtype.itemsize for a in operands) + sum(
        o.size * o.dtype.itemsize for o in outs
    )
    return pl.pallas_call(
        kernel,
        out_shape=tuple(outs),
        in_specs=specs or [VMEM] * len(operands),
        out_specs=(out_spec,) * len(outs),
        scratch_shapes=list(scratch),
        compiler_params=pltpu.CompilerParams(vmem_limit_bytes=VMEM_LIMIT),
        cost_estimate=pl.CostEstimate(flops=int(COSTS[getattr(kernel, "func", kernel)] * 1.15e9), bytes_accessed=0, transcendentals=0),
    )(*operands)


def shaped(*shape, dtype=BF16):
    return jax.ShapeDtypeStruct(shape, dtype)


def tie(value, *after):
    return lax.optimization_barrier((value, *after))[0]


class Group:
    def __init__(self, m, d):
        self.m, self.d = m, d
        self.j, self.c, self.z = (lax.axis_index(axis) for axis in AXES)
        self.pos = jnp.stack([self.j, self.c, self.z]).astype(jnp.int32)

    def plane(self, value, r):
        return lax.ppermute(value, "j", [(i, i ^ r) for i in range(PLANE)])

    def core(self, value, k):
        return lax.ppermute(value, "c", [(i, (i + k) % self.m) for i in range(self.m)])

    def everyone(self, value, step):
        n = PLANE * self.m * self.d
        return value + lax.ppermute(value, AXES, [(i, i ^ step) for i in range(n)])


def plane_near(grp, own):
    return [own, grp.plane(own, 1), grp.plane(own, 2)]


def plane_far(grp, near, *after):
    own, one, two = near
    half = own.shape[0] // 2
    top, low = grp.plane(one[:half], 2), grp.plane(two[half:], 1)
    if after:
        top, low = tie(top, *after), tie(low, *after)
    return [own, one, two, jnp.concatenate([top, low], axis=0)]


def plane_gather(grp, own):
    return plane_far(grp, plane_near(grp, own))


def plane_send(grp, parts):
    return [parts[0]] + [grp.plane(parts[r], r) for r in range(1, PLANE)]


def plane_scatter_second(grp, part, axis, got):
    sent = add_up([part, got[part.shape[0] :]]).astype(BF16)
    return sent, grp.plane(sent, 3 - axis)


def add_up(terms):
    return sum(term.astype(F32) for term in terms)


def exchange(grp, pieces):
    return [pieces[0]] + [grp.plane(pieces[r], r) for r in range(1, PLANE)]


def core_terms(grp, halves):
    return [halves[0]] + [grp.core(halves[k], k) for k in range(1, grp.m)]


def owner(grp, kernel, message, piece, rest=()):
    return call(
        kernel,
        (shaped(*piece),) * PLANE + rest,
        (grp.pos, message),
        specs=[SMEM, VMEM],
    )


def weight_grad(grp, lefts, rights, lead):
    length, rows = lefts[0].shape
    columns = rights[0].shape[1]
    share = rows // lead // grp.m
    return call(
        functools.partial(weight_grad_kernel, grp.m),
        (shaped(lead, share, columns),) * grp.m,
        (grp.pos, *lefts, *rights),
        scratch=(
            pltpu.VMEM((PLANE * length, rows), BF16),
            pltpu.VMEM((PLANE * length, columns), BF16),
            pltpu.VMEM((rows // lead, columns), F32),
            pltpu.SemaphoreType.DMA((2 * PLANE,)),
        ),
        specs=[SMEM] + [ANY] * (2 * PLANE),
        flops=2 * PLANE * length * rows * columns,
    )


def adam_columns(grp, pieces, weight, first, second, parts):
    rows, columns = weight.shape
    return call(
        functools.partial(adam_columns_kernel, parts, columns // parts),
        (shaped(rows, columns, dtype=F32),) * 3 + (shaped(8, rows, dtype=F32),),
        (grp.pos, *pieces, weight, first, second),
        specs=[SMEM] + [VMEM] * (PLANE + 3),
    )


def norm_back(grad_normed, values, gain):
    scale_rows = rms_scale(values)
    scaled = grad_normed * gain
    unit_rows = values * scale_rows
    return scale_rows * (
        scaled - unit_rows * jnp.mean(scaled * unit_rows, axis=-1, keepdims=True)
    )


def adam_update(weight, first, second, grad, rate, decay):
    first_new = BETA_FIRST * first + (1.0 - BETA_FIRST) * grad
    second_new = BETA_SECOND * second + (1.0 - BETA_SECOND) * grad * grad
    corrected_first = first_new / (1.0 - BETA_FIRST**STEP)
    corrected_second = second_new / (1.0 - BETA_SECOND**STEP)
    weight_new = weight - rate * (
        corrected_first / (jnp.sqrt(corrected_second) + ADAM_EPSILON) + decay * weight
    )
    return (weight_new, first_new, second_new)


def per_device(
    members,
    d,
    inputs,
    cotangent,
    needle,
    qkv_weight,
    qkv_first,
    qkv_second,
    out_weight,
    out_first,
    out_second,
    gateup_weight,
    gateup_first,
    gateup_second,
    down_weight,
    down_first,
    down_second,
    norm_gains,
    gains_first,
    gains_second,
    lambdas,
    lambdas_first,
    lambdas_second,
    head_gain,
    head_first,
    head_second,
):
    grp = Group(members, d)
    length, width = inputs.shape
    rows = qkv_weight.shape[0]

    gains_low = norm_gains.astype(BF16)
    plane_slots = jnp.stack([grp.j ^ r for r in range(PLANE)]).astype(jnp.int32)
    wide = 3 * LOCAL_Q + HEAD
    count = members * d
    everywhere = functools.partial(lax.all_gather, axis_name=("c", "dp"), axis=0, tiled=False)
    to_owner = functools.partial(lax.psum_scatter, axis_name="dp", scatter_dimension=0, tiled=False)
    late = lambda terms, *marks: [terms[0]] + [tie(term, *marks) for term in terms[1:]]
    first_quarters = call(
        functools.partial(split_kernel, 3),
        (shaped(rows, wide),) * PLANE,
        (grp.pos, qkv_weight, norm_gains),
        specs=[SMEM] + [VMEM] * 2,
    )
    first_message = call(
        message_kernel,
        (shaped(rows, PLANE * wide + width),),
        (plane_slots, *exchange(grp, first_quarters), out_weight),
        scratch=(pltpu.SemaphoreType.DMA((PLANE,)),),
        specs=[SMEM] + [ANY] * PLANE + [VMEM],
    )[0]
    second_quarters = call(
        functools.partial(split_kernel, 2),
        (shaped(rows, 2 * LOCAL_FF),) * PLANE,
        (grp.pos, tie(gateup_weight, first_quarters[0])),
        specs=[SMEM, VMEM],
    )
    second_message = call(
        stack_kernel,
        (shaped(PLANE, rows, 2 * LOCAL_FF),),
        (plane_slots, *exchange(grp, second_quarters)),
        scratch=(pltpu.SemaphoreType.DMA((PLANE,)),),
        specs=[SMEM] + [ANY] * PLANE,
    )[0]
    first_all = everywhere(first_message)
    x_near = plane_near(grp, tie(inputs, first_message))
    second_all = everywhere(tie(second_message, *x_near[1:]))
    x_blocks = plane_far(grp, x_near)
    down_all = everywhere(tie(down_weight, x_blocks[3]).astype(BF16))
    grad_out = cotangent.astype(F32) * needle.astype(F32)[:, None]
    dy_near = plane_near(grp, tie(grad_out, x_blocks[3]).astype(BF16))
    dy_blocks = plane_far(grp, dy_near)
    qkv_full, out_full, gains_full = call(
        place_first_kernel,
        (
            shaped(PLANE, count, rows, wide),
            shaped(count, rows, width),
            shaped(8, width, dtype=F32),
        ),
        (tie(first_all, x_blocks[3], *dy_near[1:]),),
        scratch=(pltpu.SemaphoreType.DMA((count * (PLANE + 1),)),),
        specs=[ANY],
    )
    qkv_full, out_full = qkv_full.reshape(width, wide), out_full.reshape(LOCAL_Q, width)
    gain_one, gain_two = gains_full[0:1], gains_full[1:2]
    first_term = jnp.exp(jnp.sum(lambdas[0] * lambdas[1]))
    second_term = jnp.exp(jnp.sum(lambdas[2] * lambdas[3]))
    mixing = first_term - second_term + LAMBDA_INIT
    lam = jnp.broadcast_to(mixing, (1, HEAD))
    hg = head_gain.reshape(1, HEAD)

    activations = inputs.astype(F32)
    normed_one, projected, merged, parts = ([None] * PLANE for _ in range(4))
    for r in (3, 1, 2, 0):
        normed_one[r], projected[r], merged[r], parts[r] = call(
            attend_kernel,
            (
                shaped(length, width),
                shaped(length, 3 * LOCAL_Q),
                shaped(length, LOCAL_Q),
                shaped(length, width),
            ),
            (x_blocks[r] if r else tie(x_blocks[r], dy_blocks[3]), gain_one, qkv_full, out_full, lam, hg),
        )
    residual = activations + add_up(plane_send(grp, parts))
    normed_two = (residual * rms_scale(residual) * gain_two).astype(BF16)

    n2_near = plane_near(grp, normed_two)
    gateup_full = call(
        place_second_kernel,
        (shaped(PLANE, count, rows, 2 * LOCAL_FF),),
        (tie(second_all, normed_two),),
        scratch=(pltpu.SemaphoreType.DMA((count,)),),
        specs=[ANY],
    )[0].reshape(width, -1)
    n2_near[1:] = [tie(block, gateup_full) for block in n2_near[1:]]
    pairs = ((0, 1), (2, 3))
    flat = lambda lists: [item for items in lists for item in items]
    hidden, gate_factor, up_factor, lefts = ([] for _ in range(4))
    n2_blocks = n2_near
    for pair in pairs:
        if pair[1] == 3:
            n2_blocks = plane_far(grp, n2_near, hidden[0])
        h, gate, up, *columns = call(
            functools.partial(hidden_kernel, 2, members),
            (shaped(2 * length, LOCAL_FF),) * 3
            + (shaped(2 * length, width // members),) * members,
            (grp.pos, *(n2_blocks[r] for r in pair), gateup_full),
            specs=[SMEM] + [VMEM] * 3,
        )
        hidden.append(h)
        gate_factor.append(gate)
        up_factor.append(up)
        lefts.append(core_terms(grp, columns))

    down_halves = call(
        functools.partial(down_grad_kernel, 2, members),
        (shaped(LOCAL_FF // members, width),) * members,
        (grp.pos, *hidden, *dy_blocks),
        specs=[SMEM] + [VMEM] * (2 + PLANE),
    )
    down_full = tie(down_all, down_halves[0]).reshape(LOCAL_FF, width)
    dn2_terms, rights = [None] * PLANE, [None] * 2
    for i in (1, 0):
        pair = pairs[i]
        *sent, grad = call(
            functools.partial(hidden_back_kernel, 2),
            (shaped(length, width),) * 2 + (shaped(2 * length, 2 * LOCAL_FF),),
            (
                *(dy_blocks[r] for r in pair),
                tie(gate_factor[i], *flat(lefts)) if i else gate_factor[i],
                up_factor[i],
                gateup_full,
                down_full,
            ),
        )
        rights[i] = [grad] + [grp.core(grad, k) for k in range(1, members)]
        for r, block in zip(pair, sent):
            dn2_terms[r] = grp.plane(block, r) if r else block
    down_terms = core_terms(grp, down_halves)
    second_message = call(
        functools.partial(second_grad_kernel, 2 * members, members),
        (shaped(d, PLANE * rows + down_weight.shape[0] * 3 // 4, 2 * LOCAL_FF),),
        (*flat(lefts), *flat(rights), *down_terms),
    )[0]
    second_sum = to_owner(second_message)
    grad_residual = grad_out + norm_back(
        add_up(late(dn2_terms, second_message)), residual, gain_two
    )

    dh_near = plane_near(grp, grad_residual.astype(BF16))
    dh_blocks = plane_far(grp, dh_near)
    y_parts = call(
        functools.partial(down_kernel, 2),
        (shaped(length, width),) * 2 + (shaped(2 * length, width),),
        (*hidden, tie(down_full, grad_residual)),
    )
    dp_blocks, dn1_parts, stats = ([None] * PLANE for _ in range(3))
    for r in range(PLANE):
        block = tie(dh_blocks[r], dp_blocks[r - 1] if r else y_parts[0])
        dp_blocks[r], dn1_parts[r], stats[r] = call(
            attend_back_kernel,
            (
                shaped(length, 3 * LOCAL_Q),
                shaped(length, width),
                shaped(2, HEAD, dtype=F32),
            ),
            (block, projected[r], qkv_full, out_full, lam, hg),
            scratch=(pltpu.VMEM((length, LOCAL_Q), F32),),
        )
    half = PLANE * count // 2
    stat = grp.everyone(grp.everyone(add_up(stats), half), half // 2)
    y_got = grp.plane(tie(y_parts[2], stat), 1)
    qkv_halves = weight_grad(grp, normed_one, dp_blocks, PLANE)
    out_halves = weight_grad(grp, [tie(merged[0], stat), *merged[1:]], dh_blocks, 1)
    dn1_got = grp.plane(tie(jnp.concatenate([dn1_parts[2], dn1_parts[3]], axis=0), stat), 2)
    step = half // 4
    while step:
        stat = grp.everyone(stat, step)
        step //= 2
    first_chunks = call(
        functools.partial(chunk_first_kernel, members),
        (shaped(d, rows, PLANE * 3 * LOCAL_Q + width),),
        (*core_terms(grp, qkv_halves), *core_terms(grp, out_halves)),
    )[0]
    first_sum = to_owner(first_chunks)

    *gateup_pieces, down_grad = owner(
        grp,
        owner_second_kernel,
        tie(second_sum, first_chunks),
        (rows, 2 * LOCAL_FF),
        (shaped(*down_weight.shape, dtype=F32),),
    )
    gateup_pieces = exchange(grp, gateup_pieces)
    y_got = tie(y_got, gateup_pieces[0])
    y_sent, y_last = plane_scatter_second(grp, y_parts[1], 1, y_got)
    dn1_got = tie(dn1_got, y_sent, *gateup_pieces[1:])
    dn1_sent, dn1_last = plane_scatter_second(grp, dn1_parts[1], 2, dn1_got)
    *gateup_res, gateup_dot = adam_columns(
        grp, late(gateup_pieces, dn1_sent), gateup_weight, gateup_first, gateup_second, 2
    )
    *qkv_pieces, out_grad = owner(
        grp,
        owner_first_kernel,
        tie(first_sum, gateup_dot, stat),
        (rows, 3 * LOCAL_Q),
        (shaped(*out_weight.shape, dtype=F32),),
    )
    qkv_pieces = exchange(grp, qkv_pieces)
    y_got, y_last = tie(y_got, qkv_pieces[0]), tie(y_last, qkv_pieces[0])
    layer_output = (residual + add_up([y_parts[0], y_got[:length], y_last])).astype(BF16)
    dn1_got, dn1_last = tie(dn1_got, layer_output), tie(dn1_last, layer_output)
    input_grad = grad_residual + norm_back(
        add_up([dn1_parts[0], dn1_got[:length], dn1_last]), activations, gain_one
    )
    *qkv_res, qkv_dot = adam_columns(
        grp, late(qkv_pieces, input_grad), qkv_weight, qkv_first, qkv_second, 3
    )
    total_head, total_mixing = stat[0], stat[1, 0]
    gains_grad = jnp.concatenate([qkv_dot[:1], gateup_dot[:1]]) / gains_low.astype(F32)
    lambdas_grad = jnp.stack(
        [
            total_mixing * first_term * lambdas[1],
            total_mixing * first_term * lambdas[0],
            -total_mixing * second_term * lambdas[3],
            -total_mixing * second_term * lambdas[2],
        ]
    )
    out_res = adam_update(out_weight, out_first, out_second, out_grad, RATE_MATRIX, WEIGHT_DECAY)
    down_res = adam_update(
        down_weight, down_first, down_second, down_grad, RATE_MATRIX, WEIGHT_DECAY
    )
    gains_res = adam_update(norm_gains, gains_first, gains_second, gains_grad, RATE_GAIN, 0.0)
    lambdas_res = adam_update(
        lambdas, lambdas_first, lambdas_second, lambdas_grad, RATE_LAMBDA, 0.0
    )
    head_res = adam_update(head_gain, head_first, head_second, total_head, RATE_GAIN, 0.0)
    return (
        layer_output,
        input_grad,
        *qkv_res,
        *out_res,
        *gateup_res,
        *down_res,
        *gains_res,
        *lambdas_res,
        *head_res,
    )


def solution(mesh):
    members, d = mesh.shape["fsdp"] // PLANE, mesh.shape["dp"]
    inner = Mesh(mesh.devices.reshape(PLANE, members, d), AXES)
    rows, cols, whole = P(AXES, None), P(None, AXES), P()
    return jax.shard_map(
        functools.partial(per_device, members, d),
        mesh=inner,
        in_specs=(rows, rows, P(AXES)) + (rows,) * 12 + (cols,) * 3 + (whole,) * 6,
        out_specs=(rows,) * 14 + (cols,) * 3 + (whole,) * 6,
        check_vma=False,
    )
```

```python
import functools

import jax
import jax.numpy as jnp
from jax import lax
from jax.experimental import pallas as pl
from jax.experimental.pallas import tpu as pltpu
from jax.sharding import Mesh
from jax.sharding import PartitionSpec as P

HEADS = 12
HDIM = 64
HEAD = 2 * HDIM
FF = 4096
STEP = 10
PLANE = 4
LOCAL_HEADS = HEADS // PLANE
LOCAL_FF = FF // PLANE
LOCAL_Q = LOCAL_HEADS * HEAD

NORM_EPSILON = 1e-05
LAMBDA_INIT = 0.2
FACTOR = 1.0 - LAMBDA_INIT
BETA_FIRST = 0.9
BETA_SECOND = 0.95
ADAM_EPSILON = 1e-08
WEIGHT_DECAY = 0.1
RATE_MATRIX = 0.02
RATE_GAIN = 0.5
RATE_LAMBDA = 0.15
MASKED = -1000000000.0
SCALE = HDIM ** (-0.5)

BF16 = jnp.bfloat16
F32 = jnp.float32
VMEM_LIMIT = 28 * 1024 * 1024
AXES = ("j", "c", "dp")


def rms_scale(values):
    return lax.rsqrt(jnp.mean(values * values, axis=-1, keepdims=True) + NORM_EPSILON)


def mm(left, right):
    return lax.dot_general(left, right, (((1,), (0,)), ((), ())), preferred_element_type=F32)


def mm_nt(left, right):
    return lax.dot_general(left, right, (((1,), (1,)), ((), ())), preferred_element_type=F32)


def mm_tn(left, right):
    return lax.dot_general(left, right, (((0,), (0,)), ((), ())), preferred_element_type=F32)


def softmax_pair(q, k, rows):
    first = lax.broadcasted_iota(jnp.int32, (rows, HEAD), 1) < HDIM
    allowed = lax.broadcasted_iota(jnp.int32, (rows, rows), 0) >= lax.broadcasted_iota(
        jnp.int32, (rows, rows), 1
    )
    zero = jnp.zeros_like(q)
    result = []
    for half in (jnp.where(first, q, zero), jnp.where(first, zero, q)):
        scores = jnp.where(allowed, mm_nt(half, k) * SCALE, MASKED)
        terms = jnp.exp(scores - jnp.max(scores, axis=-1, keepdims=True))
        result.append(terms * (1.0 / jnp.sum(terms, axis=-1, keepdims=True)))
    return result


def attend_kernel(x_ref, gain_ref, wq_ref, wo_ref, lam_ref, hg_ref, n_ref, p_ref, g_ref, o_ref):
    rows = x_ref.shape[0]
    x = x_ref[...].astype(F32)
    n_ref[...] = (x * rms_scale(x) * gain_ref[...]).astype(BF16)
    for part in range(3):
        cols = pl.ds(part * LOCAL_Q, LOCAL_Q)
        p_ref[:, cols] = mm(n_ref[...], wq_ref[:, cols]).astype(BF16)
    lam = lam_ref[0, 0]
    for head in range(LOCAL_HEADS):
        q, k, v = (
            p_ref[:, pl.ds(part * LOCAL_Q + head * HEAD, HEAD)] for part in range(3)
        )
        a1, a2 = softmax_pair(q, k, rows)
        mixed = (a1 - lam * a2).astype(BF16)
        out = mm(mixed, v)
        g_ref[:, pl.ds(head * HEAD, HEAD)] = (
            out * rms_scale(out) * hg_ref[...] * FACTOR
        ).astype(BF16)
    o_ref[...] = mm(g_ref[...], wo_ref[...]).astype(BF16)


def join(refs):
    return jnp.concatenate([ref[...] for ref in refs], axis=0)


def part_of(refs, value):
    length = refs[0].shape[0]
    for i, ref in enumerate(refs):
        ref[...] = value[i * length : (i + 1) * length]


def down_blocks(rows):
    tall, block = rows * 3 // 4, 512
    cuts = sorted({*range(0, 3 * rows + 1, rows), *range(0, 3 * rows + 1, tall)})
    for at, stop in zip(cuts, cuts[1:]):
        yield at % rows, at // rows * block, at % tall, at // tall * block, stop - at


def pick(pos, pieces, k):
    m = len(pieces)
    value = pieces[0]
    for i in range(1, m):
        value = jnp.where((pos + k) % m == i, pieces[i], value)
    return value


def hidden_kernel(count, m, pos_ref, *refs):
    n_refs, (wgu_ref, h_ref, gate_ref, up_ref, *outs) = refs[:count], refs[count:]
    normed = join(n_refs)
    gate = mm(normed, wgu_ref[:, :LOCAL_FF])
    up = mm(normed, wgu_ref[:, LOCAL_FF:])
    sig = 0.5 * jnp.tanh(0.5 * gate) + 0.5
    silu = gate * sig
    h_ref[...] = (silu * up).astype(BF16)
    gate_ref[...] = (up * (sig + silu * (1.0 - sig))).astype(BF16)
    up_ref[...] = silu.astype(BF16)
    split_columns(m, pos_ref[1], normed, outs)


def split_columns(m, c, value, outs):
    width = value.shape[1] // PLANE
    share = width // m
    for k in range(m):
        columns = []
        for j in range(PLANE):
            pieces = [
                value[:, j * width + i * share : j * width + (i + 1) * share] for i in range(m)
            ]
            columns.append(pick(c, pieces, k))
        outs[k][...] = jnp.concatenate(columns, axis=1)


def hidden_back_kernel(count, *refs):
    dy_refs, (gate_ref, up_ref, wgu_ref, wd_ref, *outs, grad_ref) = refs[:count], refs[count:]
    dh = mm_nt(join(dy_refs), wd_ref[...])
    grad_ref[:, :LOCAL_FF] = (dh * gate_ref[...].astype(F32)).astype(BF16)
    grad_ref[:, LOCAL_FF:] = (dh * up_ref[...].astype(F32)).astype(BF16)
    part_of(outs, mm_nt(grad_ref[...], wgu_ref[...]).astype(BF16))


def down_grad_kernel(count, m, pos_ref, *refs):
    h_refs, dy_refs, outs = refs[:count], refs[count:-m], refs[-m:]
    per = len(dy_refs) // count
    share = outs[0].shape[0]
    for k in range(m):
        cols = pl.ds(pl.multiple_of((pos_ref[1] + k) % m * share, HEAD), share)
        value = sum(
            mm_tn(h_refs[i][:, cols], join(dy_refs[i * per : (i + 1) * per])) for i in range(count)
        )
        outs[k][...] = value.astype(BF16)


def second_grad_kernel(count, down_terms, *refs):
    lefts, rights, downs, out = (
        refs[:count],
        refs[count : 2 * count],
        refs[2 * count : 2 * count + down_terms],
        refs[-1],
    )
    d, tile = out.shape[0], 512
    tall = downs[0].shape[0] // d
    rows = lefts[0].shape[1] // PLANE // d
    for at in range(0, rights[0].shape[1], tile):
        cols = slice(at, at + tile)
        value = sum(mm_tn(left[...], right[:, cols]) for left, right in zip(lefts, rights))
        value = value.astype(BF16)
        for z in range(d):
            for j in range(PLANE):
                start = (j * d + z) * rows
                out[z, j * rows : (j + 1) * rows, cols] = value[start : start + rows]
    for z in range(d):
        value = add_up([term[z * tall : (z + 1) * tall, :] for term in downs]).astype(BF16)
        for row, col, to_row, to_col, size in down_blocks(tall):
            out[z, PLANE * rows + to_row : PLANE * rows + to_row + size, to_col : to_col + 512] = (
                value[row : row + size, col : col + 512]
            )


def down_kernel(count, *refs):
    h_refs, wd_ref, (own_ref, two_ref, message_ref) = refs[:count], refs[count], refs[count + 1 :]
    length = own_ref.shape[0]
    for i, (even_ref, h_ref) in enumerate(zip((own_ref, two_ref), h_refs)):
        value = mm(h_ref[...], wd_ref[...]).astype(BF16)
        even_ref[...] = value[:length]
        message_ref[i * length : (i + 1) * length, :] = value[length:]


def attend_back_kernel(
    dh_ref, p_ref, wq_ref, wo_ref, lam_ref, hg_ref, dp_ref, dn_ref, stat_ref, dg_ref
):
    rows = dh_ref.shape[0]
    dg_ref[...] = mm_nt(dh_ref[...], wo_ref[...])
    lam = lam_ref[0, 0]
    hg = hg_ref[...]
    first = lax.broadcasted_iota(jnp.int32, (rows, HEAD), 1) < HDIM
    grad_hg = jnp.zeros((1, HEAD), F32)
    grad_lam = jnp.zeros((1, 1), F32)
    for head in range(LOCAL_HEADS):
        q, k, v = (
            p_ref[:, pl.ds(part * LOCAL_Q + head * HEAD, HEAD)] for part in range(3)
        )
        a1, a2 = softmax_pair(q, k, rows)
        mixed = (a1 - lam * a2).astype(BF16)
        out = mm(mixed, v)
        scale = rms_scale(out)
        unit = out * scale
        dg = dg_ref[:, pl.ds(head * HEAD, HEAD)]
        grad_hg = grad_hg + FACTOR * jnp.sum(dg * unit, axis=0, keepdims=True)
        u = dg * hg * FACTOR
        dout = (scale * (u - unit * jnp.mean(u * unit, axis=-1, keepdims=True))).astype(BF16)
        dv = mm_tn(mixed, dout)
        dm = mm_nt(dout, v)
        dot1 = jnp.sum(dm * a1, axis=-1, keepdims=True)
        dot2 = jnp.sum(dm * a2, axis=-1, keepdims=True)
        grad_lam = grad_lam - jnp.sum(dot2, axis=0, keepdims=True)
        ds1 = (a1 * (dm - dot1)).astype(BF16)
        ds2 = (-lam * a2 * (dm - dot2)).astype(BF16)
        dq = jnp.where(first, mm(ds1, k), mm(ds2, k)) * SCALE
        dk = jnp.where(first, mm_tn(ds1, q), mm_tn(ds2, q)) * SCALE
        for part, value in enumerate((dq, dk, dv)):
            dp_ref[:, pl.ds(part * LOCAL_Q + head * HEAD, HEAD)] = value.astype(BF16)
    stat_ref[0:1, :] = grad_hg
    stat_ref[1:2, :] = jnp.broadcast_to(grad_lam, (1, HEAD))
    dn_ref[...] = mm_nt(dp_ref[...], wq_ref[:, : 3 * LOCAL_Q]).astype(BF16)


def split_kernel(parts, pos_ref, w_ref, *refs):
    gain_refs, outs = refs[:-PLANE], refs[-PLANE:]
    width = w_ref.shape[1] // parts
    quarter = width // PLANE
    rows = w_ref.shape[0]
    for r, out in enumerate(outs):
        q = pos_ref[0] ^ r
        for part in range(parts):
            cols = pl.ds(pl.multiple_of(part * width + q * quarter, HEAD), quarter)
            out[:, part * quarter : (part + 1) * quarter] = w_ref[:, cols].astype(BF16)
        for gain_ref in gain_refs:
            gains = jnp.concatenate([gain_ref[...], jnp.zeros((HEAD - 2, rows), F32)], axis=0).T
            out[:, parts * quarter :] = gains.astype(BF16)


def message_kernel(slot_ref, *refs):
    pieces, (weight_ref, out_ref, sem) = refs[:PLANE], refs[PLANE:]
    wide = pieces[0].shape[1]
    copies = []
    for r in range(PLANE):
        cols = pl.ds(pl.multiple_of(slot_ref[r] * wide, HEAD), wide)
        copies.append((pieces[r], out_ref.at[:, cols]))
    copy_all(copies, sem, lambda: store_low(out_ref, PLANE * wide, weight_ref))


def stack_kernel(slot_ref, *refs):
    pieces, (out_ref, sem) = refs[:PLANE], refs[PLANE:]
    copy_all([(pieces[r], out_ref.at[slot_ref[r]]) for r in range(PLANE)], sem)


def store_low(out_ref, start, in_ref):
    out_ref[:, start:] = in_ref[...].astype(BF16)


def copy_all(pairs, sem, meanwhile=lambda: None):
    copies = [pltpu.make_async_copy(a, b, sem.at[i]) for i, (a, b) in enumerate(pairs)]
    for copy in copies:
        copy.start()
    meanwhile()
    for copy in copies:
        copy.wait()


def place_second_kernel(in_ref, out_ref, sem):
    copy_all([(in_ref.at[k], out_ref.at[:, k]) for k in range(in_ref.shape[0])], sem)


def place_first_kernel(in_ref, qkv_ref, out_ref, gain_ref, sem):
    count, (rows, wide) = in_ref.shape[0], qkv_ref.shape[2:]
    copies = []
    for k in range(count):
        for j in range(PLANE):
            copies.append((in_ref.at[k, :, pl.ds(j * wide, wide)], qkv_ref.at[j, k]))
        copies.append((in_ref.at[k, :, pl.ds(PLANE * wide, out_ref.shape[2])], out_ref.at[k]))
    copy_all(copies, sem)
    columns = qkv_ref[:, :, :, 3 * LOCAL_Q :].astype(F32).reshape(PLANE * count * rows, HEAD)
    gain_ref[...] = columns.T[:8]


def weight_grad_kernel(m, pos_ref, *refs):
    lefts, rights, outs = refs[:PLANE], refs[PLANE : 2 * PLANE], refs[2 * PLANE : 2 * PLANE + m]
    left, right, total, sem = refs[2 * PLANE + m :]
    length = lefts[0].shape[0]
    copies = []
    for r in range(PLANE):
        for i, (src, dst) in enumerate(((lefts[r], left), (rights[r], right))):
            copies.append(
                pltpu.make_async_copy(
                    src, dst.at[pl.ds(r * length, length)], sem.at[2 * r + i]
                )
            )
            copies[-1].start()
    for copy in copies:
        copy.wait()
    rows, columns = total.shape
    share = rows // m
    for lead in range(outs[0].shape[0]):
        value = mm_tn(left[:, lead * rows : (lead + 1) * rows], right[...])
        if m == 2:
            top, low = value[:share].astype(BF16), value[share:].astype(BF16)
            outs[0][lead] = jnp.where(pos_ref[1] == 0, top, low)
            outs[1][lead] = jnp.where(pos_ref[1] == 0, low, top)
        else:
            total[...] = value
            for k in range(m):
                start = pl.multiple_of(((pos_ref[1] + k) % m) * share, 8)
                outs[k][lead] = total[pl.ds(start, share), :].astype(BF16)


def chunk_first_kernel(m, *refs):
    qkv, out_terms, out = refs[:m], refs[m : 2 * m], refs[2 * m]
    d, rows, _ = out.shape
    wide = qkv[0].shape[2]
    for z in range(d):
        for j in range(PLANE + 1):
            terms, lead = (qkv, j) if j < PLANE else (out_terms, 0)
            value = add_up([term[lead, z * rows : (z + 1) * rows, :] for term in terms])
            out[z, :, j * wide : j * wide + value.shape[1]] = value.astype(BF16)


def owner_first_kernel(pos_ref, in_ref, *outs):
    *outs, out_ref = outs
    wide = outs[0].shape[1]
    for r in range(PLANE):
        outs[r][...] = in_ref[:, pl.ds(pl.multiple_of((pos_ref[0] ^ r) * wide, HEAD), wide)]
    out_ref[...] = in_ref[:, PLANE * wide :].astype(F32)


def owner_second_kernel(pos_ref, in_ref, *outs):
    *outs, down_ref = outs
    rows, tall = outs[0].shape[0], down_ref.shape[0]
    for r in range(PLANE):
        q = pos_ref[0] ^ r
        if rows % 16 == 0:
            outs[r][...] = in_ref[pl.ds(pl.multiple_of(q * rows, 16), rows), :]
        else:
            outs[r][...] = pick(q, [in_ref[i * rows : (i + 1) * rows, :] for i in range(PLANE)], 0)
    for row, col, to_row, to_col, size in down_blocks(tall):
        down_ref[row : row + size, col : col + 512] = in_ref[
            PLANE * rows + to_row : PLANE * rows + to_row + size, to_col : to_col + 512
        ].astype(F32)


def adam_columns_kernel(parts, width, pos_ref, *refs):
    pieces, (w_ref, f_ref, s_ref, wn_ref, fn_ref, sn_ref, dot_ref) = refs[:PLANE], refs[PLANE:]
    quarter = width // PLANE
    dot = jnp.zeros((w_ref.shape[0], 1), F32)
    for r in range(PLANE):
        q = pos_ref[0] ^ r
        for part in range(parts):
            cols = pl.ds(pl.multiple_of(part * width + q * quarter, HEAD), quarter)
            grad = pieces[r][:, part * quarter : (part + 1) * quarter].astype(F32)
            weight = w_ref[:, cols]
            dot = dot + jnp.sum(weight.astype(BF16).astype(F32) * grad, axis=1, keepdims=True)
            wn_ref[:, cols], fn_ref[:, cols], sn_ref[:, cols] = adam_update(
                weight, f_ref[:, cols], s_ref[:, cols], grad, RATE_MATRIX, WEIGHT_DECAY
            )
    dot_ref[...] = jnp.broadcast_to(dot, (dot.shape[0], HEAD)).T[:8]


ANY = pl.BlockSpec(memory_space=pl.ANY)
VMEM = pl.BlockSpec(memory_space=pltpu.VMEM)
SMEM = pl.BlockSpec(memory_space=pltpu.SMEM)


COSTS = {
    split_kernel: 1.0,
    message_kernel: 1.5,
    stack_kernel: 1.0,
    place_first_kernel: 2.0,
    attend_kernel: 3.5,
    place_second_kernel: 3.0,
    hidden_kernel: 5.0,
    down_grad_kernel: 4.0,
    hidden_back_kernel: 5.0,
    second_grad_kernel: 7.5,
    down_kernel: 4.5,
    attend_back_kernel: 15,
    weight_grad_kernel: 5.0,
    chunk_first_kernel: 2.0,
    owner_first_kernel: 1.0,
    owner_second_kernel: 1.0,
    adam_columns_kernel: 4.0,
}


def call(kernel, outs, operands, scratch=(), flops=0, specs=None, out_spec=VMEM):
    size = sum(a.size * a.dtype.itemsize for a in operands) + sum(
        o.size * o.dtype.itemsize for o in outs
    )
    return pl.pallas_call(
        kernel,
        out_shape=tuple(outs),
        in_specs=specs or [VMEM] * len(operands),
        out_specs=(out_spec,) * len(outs),
        scratch_shapes=list(scratch),
        compiler_params=pltpu.CompilerParams(vmem_limit_bytes=VMEM_LIMIT),
        cost_estimate=pl.CostEstimate(flops=int(COSTS[getattr(kernel, "func", kernel)] * 1.15e9), bytes_accessed=0, transcendentals=0),
    )(*operands)


def shaped(*shape, dtype=BF16):
    return jax.ShapeDtypeStruct(shape, dtype)


def tie(value, *after):
    return lax.optimization_barrier((value, *after))[0]


class Group:
    def __init__(self, m, d):
        self.m, self.d = m, d
        self.j, self.c, self.z = (lax.axis_index(axis) for axis in AXES)
        self.pos = jnp.stack([self.j, self.c, self.z]).astype(jnp.int32)

    def plane(self, value, r):
        return lax.ppermute(value, "j", [(i, i ^ r) for i in range(PLANE)])

    def core(self, value, k):
        return lax.ppermute(value, "c", [(i, (i + k) % self.m) for i in range(self.m)])

    def everyone(self, value, step):
        n = PLANE * self.m * self.d
        return value + lax.ppermute(value, AXES, [(i, i ^ step) for i in range(n)])


def plane_near(grp, own):
    return [own, grp.plane(own, 1), grp.plane(own, 2)]


def plane_far(grp, near, *after):
    own, one, two = near
    half = own.shape[0] // 2
    top, low = grp.plane(one[:half], 2), grp.plane(two[half:], 1)
    if after:
        top, low = tie(top, *after), tie(low, *after)
    return [own, one, two, jnp.concatenate([top, low], axis=0)]


def plane_gather(grp, own):
    return plane_far(grp, plane_near(grp, own))


def plane_send(grp, parts):
    return [parts[0]] + [grp.plane(parts[r], r) for r in range(1, PLANE)]


def plane_scatter_second(grp, part, axis, got):
    sent = add_up([part, got[part.shape[0] :]]).astype(BF16)
    return sent, grp.plane(sent, 3 - axis)


def add_up(terms):
    return sum(term.astype(F32) for term in terms)


def exchange(grp, pieces):
    return [pieces[0]] + [grp.plane(pieces[r], r) for r in range(1, PLANE)]


def core_terms(grp, halves):
    return [halves[0]] + [grp.core(halves[k], k) for k in range(1, grp.m)]


def owner(grp, kernel, message, piece, rest=()):
    return call(
        kernel,
        (shaped(*piece),) * PLANE + rest,
        (grp.pos, message),
        specs=[SMEM, VMEM],
    )


def weight_grad(grp, lefts, rights, lead):
    length, rows = lefts[0].shape
    columns = rights[0].shape[1]
    share = rows // lead // grp.m
    return call(
        functools.partial(weight_grad_kernel, grp.m),
        (shaped(lead, share, columns),) * grp.m,
        (grp.pos, *lefts, *rights),
        scratch=(
            pltpu.VMEM((PLANE * length, rows), BF16),
            pltpu.VMEM((PLANE * length, columns), BF16),
            pltpu.VMEM((rows // lead, columns), F32),
            pltpu.SemaphoreType.DMA((2 * PLANE,)),
        ),
        specs=[SMEM] + [ANY] * (2 * PLANE),
        flops=2 * PLANE * length * rows * columns,
    )


def adam_columns(grp, pieces, weight, first, second, parts):
    rows, columns = weight.shape
    return call(
        functools.partial(adam_columns_kernel, parts, columns // parts),
        (shaped(rows, columns, dtype=F32),) * 3 + (shaped(8, rows, dtype=F32),),
        (grp.pos, *pieces, weight, first, second),
        specs=[SMEM] + [VMEM] * (PLANE + 3),
    )


def norm_back(grad_normed, values, gain):
    scale_rows = rms_scale(values)
    scaled = grad_normed * gain
    unit_rows = values * scale_rows
    return scale_rows * (
        scaled - unit_rows * jnp.mean(scaled * unit_rows, axis=-1, keepdims=True)
    )


def adam_update(weight, first, second, grad, rate, decay):
    first_new = BETA_FIRST * first + (1.0 - BETA_FIRST) * grad
    second_new = BETA_SECOND * second + (1.0 - BETA_SECOND) * grad * grad
    corrected_first = first_new / (1.0 - BETA_FIRST**STEP)
    corrected_second = second_new / (1.0 - BETA_SECOND**STEP)
    weight_new = weight - rate * (
        corrected_first / (jnp.sqrt(corrected_second) + ADAM_EPSILON) + decay * weight
    )
    return (weight_new, first_new, second_new)


def per_device(
    members,
    d,
    inputs,
    cotangent,
    needle,
    qkv_weight,
    qkv_first,
    qkv_second,
    out_weight,
    out_first,
    out_second,
    gateup_weight,
    gateup_first,
    gateup_second,
    down_weight,
    down_first,
    down_second,
    norm_gains,
    gains_first,
    gains_second,
    lambdas,
    lambdas_first,
    lambdas_second,
    head_gain,
    head_first,
    head_second,
):
    grp = Group(members, d)
    length, width = inputs.shape
    rows = qkv_weight.shape[0]

    gains_low = norm_gains.astype(BF16)
    plane_slots = jnp.stack([grp.j ^ r for r in range(PLANE)]).astype(jnp.int32)
    wide = 3 * LOCAL_Q + HEAD
    count = members * d
    everywhere = functools.partial(lax.all_gather, axis_name=("c", "dp"), axis=0, tiled=False)
    to_owner = functools.partial(lax.psum_scatter, axis_name="dp", scatter_dimension=0, tiled=False)
    late = lambda terms, *marks: [terms[0]] + [tie(term, *marks) for term in terms[1:]]
    first_quarters = call(
        functools.partial(split_kernel, 3),
        (shaped(rows, wide),) * PLANE,
        (grp.pos, qkv_weight, norm_gains),
        specs=[SMEM] + [VMEM] * 2,
    )
    first_message = call(
        message_kernel,
        (shaped(rows, PLANE * wide + width),),
        (plane_slots, *exchange(grp, first_quarters), out_weight),
        scratch=(pltpu.SemaphoreType.DMA((PLANE,)),),
        specs=[SMEM] + [ANY] * PLANE + [VMEM],
    )[0]
    second_quarters = call(
        functools.partial(split_kernel, 2),
        (shaped(rows, 2 * LOCAL_FF),) * PLANE,
        (grp.pos, tie(gateup_weight, first_quarters[0])),
        specs=[SMEM, VMEM],
    )
    second_message = call(
        stack_kernel,
        (shaped(PLANE, rows, 2 * LOCAL_FF),),
        (plane_slots, *exchange(grp, second_quarters)),
        scratch=(pltpu.SemaphoreType.DMA((PLANE,)),),
        specs=[SMEM] + [ANY] * PLANE,
    )[0]
    first_all = everywhere(first_message)
    x_near = plane_near(grp, tie(inputs, first_message))
    second_all = everywhere(tie(second_message, *x_near[1:]))
    x_blocks = plane_far(grp, x_near)
    down_all = everywhere(tie(down_weight, x_blocks[3]).astype(BF16))
    grad_out = cotangent.astype(F32) * needle.astype(F32)[:, None]
    dy_near = plane_near(grp, tie(grad_out, x_blocks[3]).astype(BF16))
    dy_blocks = plane_far(grp, dy_near)
    qkv_full, out_full, gains_full = call(
        place_first_kernel,
        (
            shaped(PLANE, count, rows, wide),
            shaped(count, rows, width),
            shaped(8, width, dtype=F32),
        ),
        (tie(first_all, x_blocks[3], *dy_near[1:]),),
        scratch=(pltpu.SemaphoreType.DMA((count * (PLANE + 1),)),),
        specs=[ANY],
    )
    qkv_full, out_full = qkv_full.reshape(width, wide), out_full.reshape(LOCAL_Q, width)
    gain_one, gain_two = gains_full[0:1], gains_full[1:2]
    first_term = jnp.exp(jnp.sum(lambdas[0] * lambdas[1]))
    second_term = jnp.exp(jnp.sum(lambdas[2] * lambdas[3]))
    mixing = first_term - second_term + LAMBDA_INIT
    lam = jnp.broadcast_to(mixing, (1, HEAD))
    hg = head_gain.reshape(1, HEAD)

    activations = inputs.astype(F32)
    normed_one, projected, merged, parts = ([None] * PLANE for _ in range(4))
    for r in (3, 1, 2, 0):
        normed_one[r], projected[r], merged[r], parts[r] = call(
            attend_kernel,
            (
                shaped(length, width),
                shaped(length, 3 * LOCAL_Q),
                shaped(length, LOCAL_Q),
                shaped(length, width),
            ),
            (x_blocks[r] if r else tie(x_blocks[r], dy_blocks[3]), gain_one, qkv_full, out_full, lam, hg),
        )
    residual = activations + add_up(plane_send(grp, parts))
    normed_two = (residual * rms_scale(residual) * gain_two).astype(BF16)

    n2_near = plane_near(grp, normed_two)
    gateup_full = call(
        place_second_kernel,
        (shaped(PLANE, count, rows, 2 * LOCAL_FF),),
        (tie(second_all, normed_two),),
        scratch=(pltpu.SemaphoreType.DMA((count,)),),
        specs=[ANY],
    )[0].reshape(width, -1)
    n2_near[1:] = [tie(block, gateup_full) for block in n2_near[1:]]
    pairs = ((0, 1), (2, 3))
    flat = lambda lists: [item for items in lists for item in items]
    hidden, gate_factor, up_factor, lefts = ([] for _ in range(4))
    n2_blocks = n2_near
    for pair in pairs:
        if pair[1] == 3:
            n2_blocks = plane_far(grp, n2_near, hidden[0])
        h, gate, up, *columns = call(
            functools.partial(hidden_kernel, 2, members),
            (shaped(2 * length, LOCAL_FF),) * 3
            + (shaped(2 * length, width // members),) * members,
            (grp.pos, *(n2_blocks[r] for r in pair), gateup_full),
            specs=[SMEM] + [VMEM] * 3,
        )
        hidden.append(h)
        gate_factor.append(gate)
        up_factor.append(up)
        lefts.append(core_terms(grp, columns))

    down_halves = call(
        functools.partial(down_grad_kernel, 2, members),
        (shaped(LOCAL_FF // members, width),) * members,
        (grp.pos, *hidden, *dy_blocks),
        specs=[SMEM] + [VMEM] * (2 + PLANE),
    )
    down_full = tie(down_all, down_halves[0]).reshape(LOCAL_FF, width)
    dn2_terms, rights = [None] * PLANE, [None] * 2
    for i in (1, 0):
        pair = pairs[i]
        *sent, grad = call(
            functools.partial(hidden_back_kernel, 2),
            (shaped(length, width),) * 2 + (shaped(2 * length, 2 * LOCAL_FF),),
            (
                *(dy_blocks[r] for r in pair),
                tie(gate_factor[i], *flat(lefts)) if i else gate_factor[i],
                up_factor[i],
                gateup_full,
                down_full,
            ),
        )
        rights[i] = [grad] + [grp.core(grad, k) for k in range(1, members)]
        for r, block in zip(pair, sent):
            dn2_terms[r] = grp.plane(block, r) if r else block
    down_terms = core_terms(grp, down_halves)
    second_message = call(
        functools.partial(second_grad_kernel, 2 * members, members),
        (shaped(d, PLANE * rows + down_weight.shape[0] * 3 // 4, 2 * LOCAL_FF),),
        (*flat(lefts), *flat(rights), *down_terms),
    )[0]
    second_sum = to_owner(second_message)
    grad_residual = grad_out + norm_back(
        add_up(late(dn2_terms, second_message)), residual, gain_two
    )

    dh_near = plane_near(grp, grad_residual.astype(BF16))
    dh_blocks = plane_far(grp, dh_near)
    y_parts = call(
        functools.partial(down_kernel, 2),
        (shaped(length, width),) * 2 + (shaped(2 * length, width),),
        (*hidden, tie(down_full, grad_residual)),
    )
    dp_blocks, dn1_parts, stats = ([None] * PLANE for _ in range(3))
    for r in range(PLANE):
        block = tie(dh_blocks[r], dp_blocks[r - 1] if r else y_parts[0])
        dp_blocks[r], dn1_parts[r], stats[r] = call(
            attend_back_kernel,
            (
                shaped(length, 3 * LOCAL_Q),
                shaped(length, width),
                shaped(2, HEAD, dtype=F32),
            ),
            (block, projected[r], qkv_full, out_full, lam, hg),
            scratch=(pltpu.VMEM((length, LOCAL_Q), F32),),
        )
    half = PLANE * count // 2
    stat = grp.everyone(add_up(stats), half)
    qkv_halves = weight_grad(grp, normed_one, dp_blocks, PLANE)
    out_halves = weight_grad(grp, [tie(merged[0], stat), *merged[1:]], dh_blocks, 1)
    stat = grp.everyone(stat, half // 2)
    y_got = grp.plane(tie(y_parts[2], stat), 1)
    dn1_message = jnp.concatenate([dn1_parts[2], dn1_parts[3]], axis=0)
    dn1_got = grp.plane(dn1_message, 2)
    first_chunks = call(
        functools.partial(chunk_first_kernel, members),
        (shaped(d, rows, PLANE * 3 * LOCAL_Q + width),),
        (*core_terms(grp, qkv_halves), *late(core_terms(grp, out_halves), dn1_message, stat)),
    )[0]
    first_sum = to_owner(first_chunks)

    *gateup_pieces, down_grad = owner(
        grp,
        owner_second_kernel,
        tie(second_sum, first_chunks),
        (rows, 2 * LOCAL_FF),
        (shaped(*down_weight.shape, dtype=F32),),
    )
    stat = tie(stat, gateup_pieces[0])
    step = half // 4
    while step:
        stat = grp.everyone(stat, step)
        step //= 2
    gateup_pieces = exchange(grp, gateup_pieces)
    y_got = tie(y_got, gateup_pieces[0])
    y_sent, y_last = plane_scatter_second(grp, y_parts[1], 1, y_got)
    dn1_got = tie(dn1_got, y_sent, *gateup_pieces[1:])
    dn1_sent, dn1_last = plane_scatter_second(grp, dn1_parts[1], 2, dn1_got)
    *gateup_res, gateup_dot = adam_columns(
        grp, late(gateup_pieces, dn1_sent), gateup_weight, gateup_first, gateup_second, 2
    )
    *qkv_pieces, out_grad = owner(
        grp,
        owner_first_kernel,
        tie(first_sum, gateup_dot, stat),
        (rows, 3 * LOCAL_Q),
        (shaped(*out_weight.shape, dtype=F32),),
    )
    qkv_pieces = exchange(grp, qkv_pieces)
    y_got, y_last = tie(y_got, qkv_pieces[0]), tie(y_last, qkv_pieces[0])
    layer_output = (residual + add_up([y_parts[0], y_got[:length], y_last])).astype(BF16)
    dn1_got, dn1_last = tie(dn1_got, layer_output), tie(dn1_last, layer_output)
    input_grad = grad_residual + norm_back(
        add_up([dn1_parts[0], dn1_got[:length], dn1_last]), activations, gain_one
    )
    *qkv_res, qkv_dot = adam_columns(
        grp, late(qkv_pieces, input_grad), qkv_weight, qkv_first, qkv_second, 3
    )
    total_head, total_mixing = stat[0], stat[1, 0]
    gains_grad = jnp.concatenate([qkv_dot[:1], gateup_dot[:1]]) / gains_low.astype(F32)
    lambdas_grad = jnp.stack(
        [
            total_mixing * first_term * lambdas[1],
            total_mixing * first_term * lambdas[0],
            -total_mixing * second_term * lambdas[3],
            -total_mixing * second_term * lambdas[2],
        ]
    )
    out_res = adam_update(out_weight, out_first, out_second, out_grad, RATE_MATRIX, WEIGHT_DECAY)
    down_res = adam_update(
        down_weight, down_first, down_second, down_grad, RATE_MATRIX, WEIGHT_DECAY
    )
    gains_res = adam_update(norm_gains, gains_first, gains_second, gains_grad, RATE_GAIN, 0.0)
    lambdas_res = adam_update(
        lambdas, lambdas_first, lambdas_second, lambdas_grad, RATE_LAMBDA, 0.0
    )
    head_res = adam_update(head_gain, head_first, head_second, total_head, RATE_GAIN, 0.0)
    return (
        layer_output,
        input_grad,
        *qkv_res,
        *out_res,
        *gateup_res,
        *down_res,
        *gains_res,
        *lambdas_res,
        *head_res,
    )


def solution(mesh):
    members, d = mesh.shape["fsdp"] // PLANE, mesh.shape["dp"]
    inner = Mesh(mesh.devices.reshape(PLANE, members, d), AXES)
    rows, cols, whole = P(AXES, None), P(None, AXES), P()
    return jax.shard_map(
        functools.partial(per_device, members, d),
        mesh=inner,
        in_specs=(rows, rows, P(AXES)) + (rows,) * 12 + (cols,) * 3 + (whole,) * 6,
        out_specs=(rows,) * 14 + (cols,) * 3 + (whole,) * 6,
        check_vma=False,
    )
```

```python
import functools

import jax
import jax.numpy as jnp
from jax import lax
from jax.experimental import pallas as pl
from jax.experimental.pallas import tpu as pltpu
from jax.sharding import Mesh
from jax.sharding import PartitionSpec as P

HEADS = 12
HDIM = 64
HEAD = 2 * HDIM
FF = 4096
STEP = 10
PLANE = 4
LOCAL_HEADS = HEADS // PLANE
LOCAL_FF = FF // PLANE
LOCAL_Q = LOCAL_HEADS * HEAD

NORM_EPSILON = 1e-05
LAMBDA_INIT = 0.2
FACTOR = 1.0 - LAMBDA_INIT
BETA_FIRST = 0.9
BETA_SECOND = 0.95
ADAM_EPSILON = 1e-08
WEIGHT_DECAY = 0.1
RATE_MATRIX = 0.02
RATE_GAIN = 0.5
RATE_LAMBDA = 0.15
MASKED = -1000000000.0
SCALE = HDIM ** (-0.5)

BF16 = jnp.bfloat16
F32 = jnp.float32
VMEM_LIMIT = 28 * 1024 * 1024
AXES = ("j", "c", "dp")


def rms_scale(values):
    return lax.rsqrt(jnp.mean(values * values, axis=-1, keepdims=True) + NORM_EPSILON)


def mm(left, right):
    return lax.dot_general(left, right, (((1,), (0,)), ((), ())), preferred_element_type=F32)


def mm_nt(left, right):
    return lax.dot_general(left, right, (((1,), (1,)), ((), ())), preferred_element_type=F32)


def mm_tn(left, right):
    return lax.dot_general(left, right, (((0,), (0,)), ((), ())), preferred_element_type=F32)


def softmax_pair(q, k, rows):
    first = lax.broadcasted_iota(jnp.int32, (rows, HEAD), 1) < HDIM
    allowed = lax.broadcasted_iota(jnp.int32, (rows, rows), 0) >= lax.broadcasted_iota(
        jnp.int32, (rows, rows), 1
    )
    zero = jnp.zeros_like(q)
    result = []
    for half in (jnp.where(first, q, zero), jnp.where(first, zero, q)):
        scores = jnp.where(allowed, mm_nt(half, k) * SCALE, MASKED)
        terms = jnp.exp(scores - jnp.max(scores, axis=-1, keepdims=True))
        result.append(terms * (1.0 / jnp.sum(terms, axis=-1, keepdims=True)))
    return result


def attend_kernel(x_ref, gain_ref, wq_ref, wo_ref, lam_ref, hg_ref, n_ref, p_ref, g_ref, o_ref):
    rows = x_ref.shape[0]
    x = x_ref[...].astype(F32)
    n_ref[...] = (x * rms_scale(x) * gain_ref[...]).astype(BF16)
    for part in range(3):
        cols = pl.ds(part * LOCAL_Q, LOCAL_Q)
        p_ref[:, cols] = mm(n_ref[...], wq_ref[:, cols]).astype(BF16)
    lam = lam_ref[0, 0]
    for head in range(LOCAL_HEADS):
        q, k, v = (
            p_ref[:, pl.ds(part * LOCAL_Q + head * HEAD, HEAD)] for part in range(3)
        )
        a1, a2 = softmax_pair(q, k, rows)
        mixed = (a1 - lam * a2).astype(BF16)
        out = mm(mixed, v)
        g_ref[:, pl.ds(head * HEAD, HEAD)] = (
            out * rms_scale(out) * hg_ref[...] * FACTOR
        ).astype(BF16)
    o_ref[...] = mm(g_ref[...], wo_ref[...]).astype(BF16)


def join(refs):
    return jnp.concatenate([ref[...] for ref in refs], axis=0)


def part_of(refs, value):
    length = refs[0].shape[0]
    for i, ref in enumerate(refs):
        ref[...] = value[i * length : (i + 1) * length]


def down_blocks(rows):
    tall, block = rows * 3 // 4, 512
    cuts = sorted({*range(0, 3 * rows + 1, rows), *range(0, 3 * rows + 1, tall)})
    for at, stop in zip(cuts, cuts[1:]):
        yield at % rows, at // rows * block, at % tall, at // tall * block, stop - at


def pick(pos, pieces, k):
    m = len(pieces)
    value = pieces[0]
    for i in range(1, m):
        value = jnp.where((pos + k) % m == i, pieces[i], value)
    return value


def hidden_kernel(count, m, pos_ref, *refs):
    n_refs, (wgu_ref, h_ref, gate_ref, up_ref, *outs) = refs[:count], refs[count:]
    normed = join(n_refs)
    gate = mm(normed, wgu_ref[:, :LOCAL_FF])
    up = mm(normed, wgu_ref[:, LOCAL_FF:])
    sig = 0.5 * jnp.tanh(0.5 * gate) + 0.5
    silu = gate * sig
    h_ref[...] = (silu * up).astype(BF16)
    gate_ref[...] = (up * (sig + silu * (1.0 - sig))).astype(BF16)
    up_ref[...] = silu.astype(BF16)
    split_columns(m, pos_ref[1], normed, outs)


def split_columns(m, c, value, outs):
    width = value.shape[1] // PLANE
    share = width // m
    for k in range(m):
        columns = []
        for j in range(PLANE):
            pieces = [
                value[:, j * width + i * share : j * width + (i + 1) * share] for i in range(m)
            ]
            columns.append(pick(c, pieces, k))
        outs[k][...] = jnp.concatenate(columns, axis=1)


def hidden_back_kernel(count, *refs):
    dy_refs, (gate_ref, up_ref, wgu_ref, wd_ref, *outs, grad_ref) = refs[:count], refs[count:]
    dh = mm_nt(join(dy_refs), wd_ref[...])
    grad_ref[:, :LOCAL_FF] = (dh * gate_ref[...].astype(F32)).astype(BF16)
    grad_ref[:, LOCAL_FF:] = (dh * up_ref[...].astype(F32)).astype(BF16)
    part_of(outs, mm_nt(grad_ref[...], wgu_ref[...]).astype(BF16))


def down_grad_kernel(count, m, pos_ref, *refs):
    h_refs, dy_refs, outs = refs[:count], refs[count:-m], refs[-m:]
    per = len(dy_refs) // count
    share = outs[0].shape[0]
    for k in range(m):
        cols = pl.ds(pl.multiple_of((pos_ref[1] + k) % m * share, HEAD), share)
        value = sum(
            mm_tn(h_refs[i][:, cols], join(dy_refs[i * per : (i + 1) * per])) for i in range(count)
        )
        outs[k][...] = value.astype(BF16)


def second_grad_kernel(count, down_terms, *refs):
    lefts, rights, downs, out = (
        refs[:count],
        refs[count : 2 * count],
        refs[2 * count : 2 * count + down_terms],
        refs[-3],
    )
    held, sem = refs[-2:]
    d, tile = out.shape[0], 512
    tall = downs[0].shape[0] // d
    rows = lefts[0].shape[1] // PLANE // d
    for z in range(d):
        value = add_up([term[z * tall : (z + 1) * tall, :] for term in downs]).astype(BF16)
        for row, col, to_row, to_col, size in down_blocks(tall):
            held[z, PLANE * rows + to_row : PLANE * rows + to_row + size, to_col : to_col + 512] = (
                value[row : row + size, col : col + 512]
            )
    copies, whole = [], rows % 16 != 0

    def send(*at):
        copies.append(pltpu.make_async_copy(held.at[at], out.at[at], sem.at[len(copies)]))
        copies[-1].start()

    if not whole:
        send(slice(None), pl.ds(PLANE * rows, out.shape[1] - PLANE * rows))
    for at in range(0, rights[0].shape[1], tile):
        cols = slice(at, at + tile)
        value = sum(mm_tn(left[...], right[:, cols]) for left, right in zip(lefts, rights))
        value = value.astype(BF16)
        for z in range(d):
            for j in range(PLANE):
                start = (j * d + z) * rows
                held[z, j * rows : (j + 1) * rows, cols] = value[start : start + rows]
        if not whole:
            send(slice(None), pl.ds(0, PLANE * rows), pl.ds(at, tile))
    if whole:
        send(slice(None))
    for copy in copies:
        copy.wait()


def down_kernel(count, *refs):
    h_refs, wd_ref, (own_ref, two_ref, message_ref) = refs[:count], refs[count], refs[count + 1 :]
    length = own_ref.shape[0]
    for i, (even_ref, h_ref) in enumerate(zip((own_ref, two_ref), h_refs)):
        value = mm(h_ref[...], wd_ref[...]).astype(BF16)
        even_ref[...] = value[:length]
        message_ref[i * length : (i + 1) * length, :] = value[length:]


def attend_back_kernel(
    dh_ref, p_ref, wq_ref, wo_ref, lam_ref, hg_ref, dp_ref, dn_ref, stat_ref, dg_ref
):
    rows = dh_ref.shape[0]
    dg_ref[...] = mm_nt(dh_ref[...], wo_ref[...])
    lam = lam_ref[0, 0]
    hg = hg_ref[...]
    first = lax.broadcasted_iota(jnp.int32, (rows, HEAD), 1) < HDIM
    grad_hg = jnp.zeros((1, HEAD), F32)
    grad_lam = jnp.zeros((1, 1), F32)
    for head in range(LOCAL_HEADS):
        q, k, v = (
            p_ref[:, pl.ds(part * LOCAL_Q + head * HEAD, HEAD)] for part in range(3)
        )
        a1, a2 = softmax_pair(q, k, rows)
        mixed = (a1 - lam * a2).astype(BF16)
        out = mm(mixed, v)
        scale = rms_scale(out)
        unit = out * scale
        dg = dg_ref[:, pl.ds(head * HEAD, HEAD)]
        grad_hg = grad_hg + FACTOR * jnp.sum(dg * unit, axis=0, keepdims=True)
        u = dg * hg * FACTOR
        dout = (scale * (u - unit * jnp.mean(u * unit, axis=-1, keepdims=True))).astype(BF16)
        dv = mm_tn(mixed, dout)
        dm = mm_nt(dout, v)
        dot1 = jnp.sum(dm * a1, axis=-1, keepdims=True)
        dot2 = jnp.sum(dm * a2, axis=-1, keepdims=True)
        grad_lam = grad_lam - jnp.sum(dot2, axis=0, keepdims=True)
        ds1 = (a1 * (dm - dot1)).astype(BF16)
        ds2 = (-lam * a2 * (dm - dot2)).astype(BF16)
        dq = jnp.where(first, mm(ds1, k), mm(ds2, k)) * SCALE
        dk = jnp.where(first, mm_tn(ds1, q), mm_tn(ds2, q)) * SCALE
        for part, value in enumerate((dq, dk, dv)):
            dp_ref[:, pl.ds(part * LOCAL_Q + head * HEAD, HEAD)] = value.astype(BF16)
    stat_ref[0:1, :] = grad_hg
    stat_ref[1:2, :] = jnp.broadcast_to(grad_lam, (1, HEAD))
    dn_ref[...] = mm_nt(dp_ref[...], wq_ref[:, : 3 * LOCAL_Q]).astype(BF16)


def split_kernel(parts, pos_ref, w_ref, *refs):
    gain_refs, outs = refs[:-PLANE], refs[-PLANE:]
    width = w_ref.shape[1] // parts
    quarter = width // PLANE
    rows = w_ref.shape[0]
    for r, out in enumerate(outs):
        q = pos_ref[0] ^ r
        for part in range(parts):
            cols = pl.ds(pl.multiple_of(part * width + q * quarter, HEAD), quarter)
            out[:, part * quarter : (part + 1) * quarter] = w_ref[:, cols].astype(BF16)
        for gain_ref in gain_refs:
            gains = jnp.concatenate([gain_ref[...], jnp.zeros((HEAD - 2, rows), F32)], axis=0).T
            out[:, parts * quarter :] = gains.astype(BF16)


def message_kernel(slot_ref, *refs):
    pieces, (weight_ref, out_ref, sem) = refs[:PLANE], refs[PLANE:]
    wide = pieces[0].shape[1]
    copies = []
    for r in range(PLANE):
        cols = pl.ds(pl.multiple_of(slot_ref[r] * wide, HEAD), wide)
        copies.append((pieces[r], out_ref.at[:, cols]))
    copy_all(copies, sem, lambda: store_low(out_ref, PLANE * wide, weight_ref))


def stack_kernel(slot_ref, *refs):
    pieces, (out_ref, sem) = refs[:PLANE], refs[PLANE:]
    copy_all([(pieces[r], out_ref.at[slot_ref[r]]) for r in range(PLANE)], sem)


def store_low(out_ref, start, in_ref):
    out_ref[:, start:] = in_ref[...].astype(BF16)


def copy_all(pairs, sem, meanwhile=lambda: None):
    copies = [pltpu.make_async_copy(a, b, sem.at[i]) for i, (a, b) in enumerate(pairs)]
    for copy in copies:
        copy.start()
    meanwhile()
    for copy in copies:
        copy.wait()


def place_second_kernel(in_ref, out_ref, sem):
    copy_all([(in_ref.at[k], out_ref.at[:, k]) for k in range(in_ref.shape[0])], sem)


def place_first_kernel(in_ref, qkv_ref, out_ref, gain_ref, sem):
    count, (rows, wide) = in_ref.shape[0], qkv_ref.shape[2:]
    copies = []
    for k in range(count):
        for j in range(PLANE):
            copies.append((in_ref.at[k, :, pl.ds(j * wide, wide)], qkv_ref.at[j, k]))
        copies.append((in_ref.at[k, :, pl.ds(PLANE * wide, out_ref.shape[2])], out_ref.at[k]))
    copy_all(copies, sem)
    columns = qkv_ref[:, :, :, 3 * LOCAL_Q :].astype(F32).reshape(PLANE * count * rows, HEAD)
    gain_ref[...] = columns.T[:8]


def weight_grad_kernel(m, pos_ref, *refs):
    lefts, rights, outs = refs[:PLANE], refs[PLANE : 2 * PLANE], refs[2 * PLANE : 2 * PLANE + m]
    left, right, total, sem = refs[2 * PLANE + m :]
    length = lefts[0].shape[0]
    copies = []
    for r in range(PLANE):
        for i, (src, dst) in enumerate(((lefts[r], left), (rights[r], right))):
            copies.append(
                pltpu.make_async_copy(
                    src, dst.at[pl.ds(r * length, length)], sem.at[2 * r + i]
                )
            )
            copies[-1].start()
    for copy in copies:
        copy.wait()
    rows, columns = total.shape
    share = rows // m
    for lead in range(outs[0].shape[0]):
        value = mm_tn(left[:, lead * rows : (lead + 1) * rows], right[...])
        if m == 2:
            top, low = value[:share].astype(BF16), value[share:].astype(BF16)
            outs[0][lead] = jnp.where(pos_ref[1] == 0, top, low)
            outs[1][lead] = jnp.where(pos_ref[1] == 0, low, top)
        else:
            total[...] = value
            for k in range(m):
                start = pl.multiple_of(((pos_ref[1] + k) % m) * share, 8)
                outs[k][lead] = total[pl.ds(start, share), :].astype(BF16)


def chunk_first_kernel(m, *refs):
    qkv, out_terms, out = refs[:m], refs[m : 2 * m], refs[2 * m]
    d, rows, _ = out.shape
    wide = qkv[0].shape[2]
    for z in range(d):
        for j in range(PLANE + 1):
            terms, lead = (qkv, j) if j < PLANE else (out_terms, 0)
            value = add_up([term[lead, z * rows : (z + 1) * rows, :] for term in terms])
            out[z, :, j * wide : j * wide + value.shape[1]] = value.astype(BF16)


def owner_first_kernel(pos_ref, in_ref, *outs):
    *outs, out_ref = outs
    wide = outs[0].shape[1]
    for r in range(PLANE):
        outs[r][...] = in_ref[:, pl.ds(pl.multiple_of((pos_ref[0] ^ r) * wide, HEAD), wide)]
    out_ref[...] = in_ref[:, PLANE * wide :].astype(F32)


def owner_second_kernel(pos_ref, in_ref, *outs):
    *outs, down_ref = outs
    rows, tall = outs[0].shape[0], down_ref.shape[0]
    for r in range(PLANE):
        q = pos_ref[0] ^ r
        if rows % 16 == 0:
            outs[r][...] = in_ref[pl.ds(pl.multiple_of(q * rows, 16), rows), :]
        else:
            outs[r][...] = pick(q, [in_ref[i * rows : (i + 1) * rows, :] for i in range(PLANE)], 0)
    for row, col, to_row, to_col, size in down_blocks(tall):
        down_ref[row : row + size, col : col + 512] = in_ref[
            PLANE * rows + to_row : PLANE * rows + to_row + size, to_col : to_col + 512
        ].astype(F32)


def adam_columns_kernel(parts, width, pos_ref, *refs):
    pieces, (w_ref, f_ref, s_ref, wn_ref, fn_ref, sn_ref, dot_ref) = refs[:PLANE], refs[PLANE:]
    quarter = width // PLANE
    dot = jnp.zeros((w_ref.shape[0], 1), F32)
    for r in range(PLANE):
        q = pos_ref[0] ^ r
        for part in range(parts):
            cols = pl.ds(pl.multiple_of(part * width + q * quarter, HEAD), quarter)
            grad = pieces[r][:, part * quarter : (part + 1) * quarter].astype(F32)
            weight = w_ref[:, cols]
            dot = dot + jnp.sum(weight.astype(BF16).astype(F32) * grad, axis=1, keepdims=True)
            wn_ref[:, cols], fn_ref[:, cols], sn_ref[:, cols] = adam_update(
                weight, f_ref[:, cols], s_ref[:, cols], grad, RATE_MATRIX, WEIGHT_DECAY
            )
    dot_ref[...] = jnp.broadcast_to(dot, (dot.shape[0], HEAD)).T[:8]


ANY = pl.BlockSpec(memory_space=pl.ANY)
VMEM = pl.BlockSpec(memory_space=pltpu.VMEM)
SMEM = pl.BlockSpec(memory_space=pltpu.SMEM)


COSTS = {
    split_kernel: 1.0,
    message_kernel: 1.5,
    stack_kernel: 1.0,
    place_first_kernel: 2.0,
    attend_kernel: 3.5,
    place_second_kernel: 3.0,
    hidden_kernel: 5.0,
    down_grad_kernel: 4.0,
    hidden_back_kernel: 5.0,
    second_grad_kernel: 7.5,
    down_kernel: 4.5,
    attend_back_kernel: 15,
    weight_grad_kernel: 5.0,
    chunk_first_kernel: 2.0,
    owner_first_kernel: 1.0,
    owner_second_kernel: 1.0,
    adam_columns_kernel: 4.0,
}


def call(kernel, outs, operands, scratch=(), flops=0, specs=None, out_spec=VMEM):
    size = sum(a.size * a.dtype.itemsize for a in operands) + sum(
        o.size * o.dtype.itemsize for o in outs
    )
    return pl.pallas_call(
        kernel,
        out_shape=tuple(outs),
        in_specs=specs or [VMEM] * len(operands),
        out_specs=(out_spec,) * len(outs),
        scratch_shapes=list(scratch),
        compiler_params=pltpu.CompilerParams(vmem_limit_bytes=VMEM_LIMIT),
        cost_estimate=pl.CostEstimate(flops=int(COSTS[getattr(kernel, "func", kernel)] * 1.15e9), bytes_accessed=0, transcendentals=0),
    )(*operands)


def shaped(*shape, dtype=BF16):
    return jax.ShapeDtypeStruct(shape, dtype)


def tie(value, *after):
    return lax.optimization_barrier((value, *after))[0]


class Group:
    def __init__(self, m, d):
        self.m, self.d = m, d
        self.j, self.c, self.z = (lax.axis_index(axis) for axis in AXES)
        self.pos = jnp.stack([self.j, self.c, self.z]).astype(jnp.int32)

    def plane(self, value, r):
        return lax.ppermute(value, "j", [(i, i ^ r) for i in range(PLANE)])

    def core(self, value, k):
        return lax.ppermute(value, "c", [(i, (i + k) % self.m) for i in range(self.m)])

    def everyone(self, value, step):
        n = PLANE * self.m * self.d
        return value + lax.ppermute(value, AXES, [(i, i ^ step) for i in range(n)])


def plane_near(grp, own):
    return [own, grp.plane(own, 1), grp.plane(own, 2)]


def plane_far(grp, near, *after):
    own, one, two = near
    half = own.shape[0] // 2
    top, low = grp.plane(one[:half], 2), grp.plane(two[half:], 1)
    if after:
        top, low = tie(top, *after), tie(low, *after)
    return [own, one, two, jnp.concatenate([top, low], axis=0)]


def plane_gather(grp, own):
    return plane_far(grp, plane_near(grp, own))


def plane_send(grp, parts):
    return [parts[0]] + [grp.plane(parts[r], r) for r in range(1, PLANE)]


def plane_scatter_second(grp, part, axis, got):
    sent = add_up([part, got[part.shape[0] :]]).astype(BF16)
    return sent, grp.plane(sent, 3 - axis)


def add_up(terms):
    return sum(term.astype(F32) for term in terms)


def exchange(grp, pieces):
    return [pieces[0]] + [grp.plane(pieces[r], r) for r in range(1, PLANE)]


def core_terms(grp, halves):
    return [halves[0]] + [grp.core(halves[k], k) for k in range(1, grp.m)]


def owner(grp, kernel, message, piece, rest=()):
    return call(
        kernel,
        (shaped(*piece),) * PLANE + rest,
        (grp.pos, message),
        specs=[SMEM, VMEM],
    )


def weight_grad(grp, lefts, rights, lead):
    length, rows = lefts[0].shape
    columns = rights[0].shape[1]
    share = rows // lead // grp.m
    return call(
        functools.partial(weight_grad_kernel, grp.m),
        (shaped(lead, share, columns),) * grp.m,
        (grp.pos, *lefts, *rights),
        scratch=(
            pltpu.VMEM((PLANE * length, rows), BF16),
            pltpu.VMEM((PLANE * length, columns), BF16),
            pltpu.VMEM((rows // lead, columns), F32),
            pltpu.SemaphoreType.DMA((2 * PLANE,)),
        ),
        specs=[SMEM] + [ANY] * (2 * PLANE),
        flops=2 * PLANE * length * rows * columns,
    )


def adam_columns(grp, pieces, weight, first, second, parts):
    rows, columns = weight.shape
    return call(
        functools.partial(adam_columns_kernel, parts, columns // parts),
        (shaped(rows, columns, dtype=F32),) * 3 + (shaped(8, rows, dtype=F32),),
        (grp.pos, *pieces, weight, first, second),
        specs=[SMEM] + [VMEM] * (PLANE + 3),
    )


def norm_back(grad_normed, values, gain):
    scale_rows = rms_scale(values)
    scaled = grad_normed * gain
    unit_rows = values * scale_rows
    return scale_rows * (
        scaled - unit_rows * jnp.mean(scaled * unit_rows, axis=-1, keepdims=True)
    )


def adam_update(weight, first, second, grad, rate, decay):
    first_new = BETA_FIRST * first + (1.0 - BETA_FIRST) * grad
    second_new = BETA_SECOND * second + (1.0 - BETA_SECOND) * grad * grad
    corrected_first = first_new / (1.0 - BETA_FIRST**STEP)
    corrected_second = second_new / (1.0 - BETA_SECOND**STEP)
    weight_new = weight - rate * (
        corrected_first / (jnp.sqrt(corrected_second) + ADAM_EPSILON) + decay * weight
    )
    return (weight_new, first_new, second_new)


def per_device(
    members,
    d,
    inputs,
    cotangent,
    needle,
    qkv_weight,
    qkv_first,
    qkv_second,
    out_weight,
    out_first,
    out_second,
    gateup_weight,
    gateup_first,
    gateup_second,
    down_weight,
    down_first,
    down_second,
    norm_gains,
    gains_first,
    gains_second,
    lambdas,
    lambdas_first,
    lambdas_second,
    head_gain,
    head_first,
    head_second,
):
    grp = Group(members, d)
    length, width = inputs.shape
    rows = qkv_weight.shape[0]

    gains_low = norm_gains.astype(BF16)
    plane_slots = jnp.stack([grp.j ^ r for r in range(PLANE)]).astype(jnp.int32)
    wide = 3 * LOCAL_Q + HEAD
    count = members * d
    everywhere = functools.partial(lax.all_gather, axis_name=("c", "dp"), axis=0, tiled=False)
    to_owner = functools.partial(lax.psum_scatter, axis_name="dp", scatter_dimension=0, tiled=False)
    late = lambda terms, *marks: [terms[0]] + [tie(term, *marks) for term in terms[1:]]
    first_quarters = call(
        functools.partial(split_kernel, 3),
        (shaped(rows, wide),) * PLANE,
        (grp.pos, qkv_weight, norm_gains),
        specs=[SMEM] + [VMEM] * 2,
    )
    first_message = call(
        message_kernel,
        (shaped(rows, PLANE * wide + width),),
        (plane_slots, *exchange(grp, first_quarters), out_weight),
        scratch=(pltpu.SemaphoreType.DMA((PLANE,)),),
        specs=[SMEM] + [ANY] * PLANE + [VMEM],
    )[0]
    second_quarters = call(
        functools.partial(split_kernel, 2),
        (shaped(rows, 2 * LOCAL_FF),) * PLANE,
        (grp.pos, tie(gateup_weight, first_quarters[0])),
        specs=[SMEM, VMEM],
    )
    second_message = call(
        stack_kernel,
        (shaped(PLANE, rows, 2 * LOCAL_FF),),
        (plane_slots, *exchange(grp, second_quarters)),
        scratch=(pltpu.SemaphoreType.DMA((PLANE,)),),
        specs=[SMEM] + [ANY] * PLANE,
    )[0]
    first_all = everywhere(first_message)
    x_near = plane_near(grp, tie(inputs, first_message))
    second_all = everywhere(tie(second_message, *x_near[1:]))
    x_blocks = plane_far(grp, x_near)
    down_all = everywhere(tie(down_weight, x_blocks[3]).astype(BF16))
    grad_out = cotangent.astype(F32) * needle.astype(F32)[:, None]
    dy_near = plane_near(grp, tie(grad_out, x_blocks[3]).astype(BF16))
    dy_blocks = plane_far(grp, dy_near)
    qkv_full, out_full, gains_full = call(
        place_first_kernel,
        (
            shaped(PLANE, count, rows, wide),
            shaped(count, rows, width),
            shaped(8, width, dtype=F32),
        ),
        (tie(first_all, x_blocks[3], *dy_near[1:]),),
        scratch=(pltpu.SemaphoreType.DMA((count * (PLANE + 1),)),),
        specs=[ANY],
    )
    qkv_full, out_full = qkv_full.reshape(width, wide), out_full.reshape(LOCAL_Q, width)
    gain_one, gain_two = gains_full[0:1], gains_full[1:2]
    first_term = jnp.exp(jnp.sum(lambdas[0] * lambdas[1]))
    second_term = jnp.exp(jnp.sum(lambdas[2] * lambdas[3]))
    mixing = first_term - second_term + LAMBDA_INIT
    lam = jnp.broadcast_to(mixing, (1, HEAD))
    hg = head_gain.reshape(1, HEAD)

    activations = inputs.astype(F32)
    normed_one, projected, merged, parts = ([None] * PLANE for _ in range(4))
    for r in (3, 1, 2, 0):
        normed_one[r], projected[r], merged[r], parts[r] = call(
            attend_kernel,
            (
                shaped(length, width),
                shaped(length, 3 * LOCAL_Q),
                shaped(length, LOCAL_Q),
                shaped(length, width),
            ),
            (x_blocks[r] if r else tie(x_blocks[r], dy_blocks[3]), gain_one, qkv_full, out_full, lam, hg),
        )
    residual = activations + add_up(plane_send(grp, parts))
    normed_two = (residual * rms_scale(residual) * gain_two).astype(BF16)

    n2_near = plane_near(grp, normed_two)
    gateup_full = call(
        place_second_kernel,
        (shaped(PLANE, count, rows, 2 * LOCAL_FF),),
        (tie(second_all, normed_two),),
        scratch=(pltpu.SemaphoreType.DMA((count,)),),
        specs=[ANY],
    )[0].reshape(width, -1)
    n2_near[1:] = [tie(block, gateup_full) for block in n2_near[1:]]
    pairs = ((0, 1), (2, 3))
    flat = lambda lists: [item for items in lists for item in items]
    hidden, gate_factor, up_factor, lefts = ([] for _ in range(4))
    n2_blocks = n2_near
    for pair in pairs:
        if pair[1] == 3:
            n2_blocks = plane_far(grp, n2_near, hidden[0])
        h, gate, up, *columns = call(
            functools.partial(hidden_kernel, 2, members),
            (shaped(2 * length, LOCAL_FF),) * 3
            + (shaped(2 * length, width // members),) * members,
            (grp.pos, *(n2_blocks[r] for r in pair), gateup_full),
            specs=[SMEM] + [VMEM] * 3,
        )
        hidden.append(h)
        gate_factor.append(gate)
        up_factor.append(up)
        lefts.append(core_terms(grp, columns))

    down_halves = call(
        functools.partial(down_grad_kernel, 2, members),
        (shaped(LOCAL_FF // members, width),) * members,
        (grp.pos, *hidden, *dy_blocks),
        specs=[SMEM] + [VMEM] * (2 + PLANE),
    )
    down_full = tie(down_all, down_halves[0]).reshape(LOCAL_FF, width)
    dn2_terms, rights = [None] * PLANE, [None] * 2
    for i in (1, 0):
        pair = pairs[i]
        *sent, grad = call(
            functools.partial(hidden_back_kernel, 2),
            (shaped(length, width),) * 2 + (shaped(2 * length, 2 * LOCAL_FF),),
            (
                *(dy_blocks[r] for r in pair),
                tie(gate_factor[i], *flat(lefts)) if i else gate_factor[i],
                up_factor[i],
                gateup_full,
                down_full,
            ),
        )
        rights[i] = [grad] + [grp.core(grad, k) for k in range(1, members)]
        for r, block in zip(pair, sent):
            dn2_terms[r] = grp.plane(block, r) if r else block
    down_terms = core_terms(grp, down_halves)
    second_message = call(
        functools.partial(second_grad_kernel, 2 * members, members),
        (shaped(d, PLANE * rows + down_weight.shape[0] * 3 // 4, 2 * LOCAL_FF),),
        (*flat(lefts), *flat(rights), *down_terms),
        scratch=(
            pltpu.VMEM((d, PLANE * rows + down_weight.shape[0] * 3 // 4, 2 * LOCAL_FF), BF16),
            pltpu.SemaphoreType.DMA((8,)),
        ),
        out_spec=ANY,
    )[0]
    second_sum = to_owner(second_message)
    grad_residual = grad_out + norm_back(
        add_up(late(dn2_terms, second_message)), residual, gain_two
    )

    dh_near = plane_near(grp, grad_residual.astype(BF16))
    dh_blocks = plane_far(grp, dh_near)
    y_parts = call(
        functools.partial(down_kernel, 2),
        (shaped(length, width),) * 2 + (shaped(2 * length, width),),
        (*hidden, tie(down_full, grad_residual)),
    )
    dp_blocks, dn1_parts, stats = ([None] * PLANE for _ in range(3))
    for r in range(PLANE):
        block = tie(dh_blocks[r], dp_blocks[r - 1] if r else y_parts[0])
        dp_blocks[r], dn1_parts[r], stats[r] = call(
            attend_back_kernel,
            (
                shaped(length, 3 * LOCAL_Q),
                shaped(length, width),
                shaped(2, HEAD, dtype=F32),
            ),
            (block, projected[r], qkv_full, out_full, lam, hg),
            scratch=(pltpu.VMEM((length, LOCAL_Q), F32),),
        )
    half = PLANE * count // 2
    stat = grp.everyone(add_up(stats), half)
    qkv_halves = weight_grad(grp, normed_one, dp_blocks, PLANE)
    out_halves = weight_grad(grp, [tie(merged[0], stat), *merged[1:]], dh_blocks, 1)
    stat = grp.everyone(stat, half // 2)
    y_got = grp.plane(tie(y_parts[2], stat), 1)
    dn1_message = jnp.concatenate([dn1_parts[2], dn1_parts[3]], axis=0)
    dn1_got = grp.plane(dn1_message, 2)
    first_chunks = call(
        functools.partial(chunk_first_kernel, members),
        (shaped(d, rows, PLANE * 3 * LOCAL_Q + width),),
        (*core_terms(grp, qkv_halves), *late(core_terms(grp, out_halves), dn1_message, stat)),
    )[0]
    first_sum = to_owner(first_chunks)

    *gateup_pieces, down_grad = owner(
        grp,
        owner_second_kernel,
        tie(second_sum, first_chunks),
        (rows, 2 * LOCAL_FF),
        (shaped(*down_weight.shape, dtype=F32),),
    )
    stat = tie(stat, gateup_pieces[0])
    step = half // 4
    while step:
        stat = grp.everyone(stat, step)
        step //= 2
    gateup_pieces = exchange(grp, gateup_pieces)
    y_got = tie(y_got, gateup_pieces[0])
    y_sent, y_last = plane_scatter_second(grp, y_parts[1], 1, y_got)
    dn1_got = tie(dn1_got, y_sent, *gateup_pieces[1:])
    dn1_sent, dn1_last = plane_scatter_second(grp, dn1_parts[1], 2, dn1_got)
    *gateup_res, gateup_dot = adam_columns(
        grp, late(gateup_pieces, dn1_sent), gateup_weight, gateup_first, gateup_second, 2
    )
    *qkv_pieces, out_grad = owner(
        grp,
        owner_first_kernel,
        tie(first_sum, gateup_dot, stat),
        (rows, 3 * LOCAL_Q),
        (shaped(*out_weight.shape, dtype=F32),),
    )
    qkv_pieces = exchange(grp, qkv_pieces)
    y_got, y_last = tie(y_got, qkv_pieces[0]), tie(y_last, qkv_pieces[0])
    layer_output = (residual + add_up([y_parts[0], y_got[:length], y_last])).astype(BF16)
    dn1_got, dn1_last = tie(dn1_got, layer_output), tie(dn1_last, layer_output)
    input_grad = grad_residual + norm_back(
        add_up([dn1_parts[0], dn1_got[:length], dn1_last]), activations, gain_one
    )
    *qkv_res, qkv_dot = adam_columns(
        grp, late(qkv_pieces, input_grad), qkv_weight, qkv_first, qkv_second, 3
    )
    total_head, total_mixing = stat[0], stat[1, 0]
    gains_grad = jnp.concatenate([qkv_dot[:1], gateup_dot[:1]]) / gains_low.astype(F32)
    lambdas_grad = jnp.stack(
        [
            total_mixing * first_term * lambdas[1],
            total_mixing * first_term * lambdas[0],
            -total_mixing * second_term * lambdas[3],
            -total_mixing * second_term * lambdas[2],
        ]
    )
    out_res = adam_update(out_weight, out_first, out_second, out_grad, RATE_MATRIX, WEIGHT_DECAY)
    down_res = adam_update(
        down_weight, down_first, down_second, down_grad, RATE_MATRIX, WEIGHT_DECAY
    )
    gains_res = adam_update(norm_gains, gains_first, gains_second, gains_grad, RATE_GAIN, 0.0)
    lambdas_res = adam_update(
        lambdas, lambdas_first, lambdas_second, lambdas_grad, RATE_LAMBDA, 0.0
    )
    head_res = adam_update(head_gain, head_first, head_second, total_head, RATE_GAIN, 0.0)
    return (
        layer_output,
        input_grad,
        *qkv_res,
        *out_res,
        *gateup_res,
        *down_res,
        *gains_res,
        *lambdas_res,
        *head_res,
    )


def solution(mesh):
    members, d = mesh.shape["fsdp"] // PLANE, mesh.shape["dp"]
    inner = Mesh(mesh.devices.reshape(PLANE, members, d), AXES)
    rows, cols, whole = P(AXES, None), P(None, AXES), P()
    return jax.shard_map(
        functools.partial(per_device, members, d),
        mesh=inner,
        in_specs=(rows, rows, P(AXES)) + (rows,) * 12 + (cols,) * 3 + (whole,) * 6,
        out_specs=(rows,) * 14 + (cols,) * 3 + (whole,) * 6,
        check_vma=False,
    )
```
